32 devices in a mesh: section: 2 (over core), dp: 16 (over z, y, x).
Axes of the slice: x: 2, y: 2, z: 4, core: 2. Of those that a mesh axis runs over, the one named last changes fastest.
Arguments:
- node_input: bfloat16 [32768, 256], P('dp'), may hold values from -6 to 6
- edge_input: bfloat16 [262144, 256], P('dp'), may hold values from -6 to 6
- senders: int32 [262144], P('dp'), may hold values from 0 to 511
- receivers: int32 [262144], P('dp'), may hold values from 0 to 511
- node_cot: bfloat16 [32768, 256], P('dp'), may hold values from -6 to 6
- edge_cot: bfloat16 [262144, 256], P('dp'), may hold values from -6 to 6
- edge_w1: bfloat16 [2, 768, 256], P('section'), may hold values from -0.21875 to 0.21875
- edge_b1: float32 [2, 256], P('section'), may hold values from -3 to 3
- edge_w2: bfloat16 [2, 256, 256], P('section'), may hold values from -0.375 to 0.375
- edge_b2: float32 [2, 256], P('section'), may hold values from -3 to 3
- edge_gain: float32 [2, 256], P('section'), may hold values from 0.5 to 1.5
- edge_shift: float32 [2, 256], P('section'), may hold values from -3 to 3
- node_w1: bfloat16 [2, 512, 256], P('section'), may hold values from -0.25 to 0.25
- node_b1: float32 [2, 256], P('section'), may hold values from -3 to 3
- node_w2: bfloat16 [2, 256, 256], P('section'), may hold values from -0.375 to 0.375
- node_b2: float32 [2, 256], P('section'), may hold values from -3 to 3
- node_gain: float32 [2, 256], P('section'), may hold values from 0.5 to 1.5
- node_shift: float32 [2, 256], P('section'), may hold values from -3 to 3
Outputs:
- node_latents: float32 [2, 32768, 256], P('section', 'dp')
- edge_latents: float32 [2, 262144, 256], P('section', 'dp')
- node_grads: float32 [2, 32768, 256], P('section', 'dp')
- edge_grads: float32 [2, 262144, 256], P('section', 'dp')
- grad_edge_w1: float32 [2, 768, 256], P('section')
- grad_edge_b1: float32 [2, 256], P('section')
- grad_edge_w2: float32 [2, 256, 256], P('section')
- grad_edge_b2: float32 [2, 256], P('section')
- grad_edge_gain: float32 [2, 256], P('section')
- grad_edge_shift: float32 [2, 256], P('section')
- grad_node_w1: float32 [2, 512, 256], P('section')
- grad_node_b1: float32 [2, 256], P('section')
- grad_node_w2: float32 [2, 256, 256], P('section')
- grad_node_b2: float32 [2, 256], P('section')
- grad_node_gain: float32 [2, 256], P('section')
- grad_node_shift: float32 [2, 256], P('section')
The draws below stay inside these ranges and needn't reach their ends.
Inputs may be any that keep to these rules, and one draw needn't show every extreme that they name: `senders`: indices within the edge's own graph of 512 nodes. `receivers`: indices within the edge's own graph of 512 nodes.
All inputs are finite; a program needn't handle non-finite values.
Results may differ from the reference program's by a relative error of at most 0.019.
Values may be sent and summed in bfloat16 or wider, within the bound.
No kernel may reach another device: no remote copies, remote signals or barrier semaphores. Data moves between devices by JAX's collectives and lax.ppermute only.
A program may use at most 320 MiB of HBM per device.

```python
import jax
import jax.numpy as jnp
from jax import lax

LATENT = 256
MICRO = 4
NODES_MB = 512
EDGES_MB = 4096
NODES = 32768
EDGES = 262144
N_DP = 16


def plant(array, stream_key, low, high):
    index_at = [jax.random.randint(jax.random.fold_in(stream_key, axis), (), 0, length) for axis, length in enumerate(array.shape)]
    widest = array.shape.index(max(array.shape))
    neighbour = index_at[:widest] + [(index_at[widest] + 1) % array.shape[widest]] + index_at[widest + 1:]
    return array.at[tuple(index_at)].set(low).at[tuple(neighbour)].set(high)


def block_levels(own_key, shape, split, smallest, largest):
    loudness, own = 1.0, jax.random.fold_in(own_key, 6)
    for axis_at, shards_of in split:
        heights = jnp.exp(jax.random.uniform(jax.random.fold_in(own, axis_at), (shards_of,), jnp.float32, smallest / len(split), largest / len(split)))
        loudness = loudness * jnp.repeat(heights, shape[axis_at] // shards_of).reshape([-1 if axis == axis_at else 1 for axis in range(len(shape))])
    return loudness


def centred(own_key, dims, spread, reach, split=(), kind=jnp.bfloat16):
    values = jax.random.normal(own_key, dims, jnp.float32) * spread
    if len(split) > 0:
        values = block_levels(own_key, dims, split, -0.22, 0.18) * values
    return jnp.clip(values, min=-reach, max=reach).astype(kind)


def setup_inputs(seed: int = 0) -> dict:
    seeds = jax.random.split(jax.random.key(seed), 19)
    node_input = centred(seeds[0], (NODES, LATENT), 1.0, 6.0, ((0, 16),))
    edge_input = centred(seeds[1], (EDGES, LATENT), 1.0, 6.0, ((0, 16),))
    senders = plant(jax.random.randint(seeds[2], (EDGES,), 0, NODES_MB), jax.random.fold_in(seeds[2], 1), 0, NODES_MB - 1).astype(jnp.int32)
    receivers = plant(jax.random.randint(seeds[3], (EDGES,), 0, NODES_MB), jax.random.fold_in(seeds[3], 1), 0, NODES_MB - 1).astype(jnp.int32)
    node_cot = centred(seeds[4], (NODES, LATENT), 1.0, 6.0, ((0, 16),))
    edge_cot = centred(seeds[5], (EDGES, LATENT), 1.0, 6.0, ((0, 16),))
    edge_w1 = centred(seeds[6], (2, 3 * LATENT, LATENT), (3 * LATENT) ** -0.5, 0.21875, ((0, 2),))
    edge_b1 = centred(seeds[7], (2, LATENT), 0.5, 3.0, ((0, 2),), jnp.float32)
    edge_w2 = centred(seeds[8], (2, LATENT, LATENT), LATENT ** -0.5, 0.375, ((0, 2),))
    edge_b2 = centred(seeds[9], (2, LATENT), 0.5, 3.0, ((0, 2),), jnp.float32)
    edge_gain = jnp.clip(0.5 + 1.0 * jax.random.uniform(seeds[10], (2, LATENT), jnp.float32) ** block_levels(seeds[10], (2, LATENT), ((0, 2),), -0.2, 0.2), 0.5, 1.5)
    edge_shift = centred(seeds[11], (2, LATENT), 0.5, 3.0, ((0, 2),), jnp.float32)
    node_w1 = centred(seeds[12], (2, 2 * LATENT, LATENT), (2 * LATENT) ** -0.5, 0.25, ((0, 2),))
    node_b1 = centred(seeds[13], (2, LATENT), 0.5, 3.0, ((0, 2),), jnp.float32)
    node_w2 = centred(seeds[14], (2, LATENT, LATENT), LATENT ** -0.5, 0.375, ((0, 2),))
    node_b2 = centred(seeds[15], (2, LATENT), 0.5, 3.0, ((0, 2),), jnp.float32)
    node_gain = jnp.clip(0.5 + 1.0 * jax.random.uniform(seeds[16], (2, LATENT), jnp.float32) ** block_levels(seeds[16], (2, LATENT), ((0, 2),), -0.2, 0.2), 0.5, 1.5)
    node_shift = centred(seeds[17], (2, LATENT), 0.5, 3.0, ((0, 2),), jnp.float32)
    return {"node_input": node_input, "edge_input": edge_input, "senders": senders, "receivers": receivers, "node_cot": node_cot, "edge_cot": edge_cot, "edge_w1": edge_w1, "edge_b1": edge_b1, "edge_w2": edge_w2, "edge_b2": edge_b2, "edge_gain": edge_gain, "edge_shift": edge_shift, "node_w1": node_w1, "node_b1": node_b1, "node_w2": node_w2, "node_b2": node_b2, "node_gain": node_gain, "node_shift": node_shift}


@jax.custom_vjp
def low(v):
    return lax.optimization_barrier(v.astype(jnp.bfloat16)).astype(jnp.float32)

@jax.custom_vjp
def low_back(v):
    return v

def low_keep(v):
    return (low(v), None)

def low_pass(kept, grad):
    return (grad,)

def back_keep(v):
    return (v, None)

def back_low(kept, grad):
    return (low(grad),)
low.defvjp(low_keep, low_pass)
low_back.defvjp(back_keep, back_low)
EPS = 1e-05

def product(left, right):
    return jnp.dot(left, right, precision=lax.Precision.HIGHEST, preferred_element_type=jnp.float32)

def layer_norm(value, gain, shift):
    mean = lax.optimization_barrier(jnp.mean(value, axis=-1, keepdims=True))
    centered = value - mean
    var = lax.optimization_barrier(jnp.mean(centered * centered, axis=-1, keepdims=True))
    return centered * lax.rsqrt(var + EPS) * gain + shift

def one_round(weights, node, edge, sender, receiver):
    w_one, b_one, w_two, b_two, gain_e, shift_e, w_three, b_three, w_four, b_four, gain_n, shift_n = weights
    node_low = low(node)
    edge_low = low(edge)
    joined = jnp.concatenate([edge_low, node_low[sender], node_low[receiver]], axis=1)
    first_pre = low_back(product(joined, w_one) + b_one)
    act = low(jax.nn.silu(first_pre))
    second_pre = low_back(product(act, w_two) + b_two)
    message = layer_norm(second_pre, gain_e, shift_e)
    total = jax.ops.segment_sum(message, receiver, num_segments=node.shape[0])
    joined_node = jnp.concatenate([node_low, low(total)], axis=1)
    third_pre = low_back(product(joined_node, w_three) + b_three)
    act_node = low(jax.nn.silu(third_pre))
    fourth_pre = low_back(product(act_node, w_four) + b_four)
    update = layer_norm(fourth_pre, gain_n, shift_n)
    return (node + update, edge + message)

def reference(node_input, edge_input, senders, receivers, node_cot, edge_cot, edge_w1, edge_b1, edge_w2, edge_b2, edge_gain, edge_shift, node_w1, node_b1, node_w2, node_b2, node_gain, node_shift):
    graphs = N_DP * MICRO
    params = (edge_w1, edge_b1, edge_w2, edge_b2, edge_gain, edge_shift, node_w1, node_b1, node_w2, node_b2, node_gain, node_shift)
    round_one = tuple((p[0].astype(jnp.float32) for p in params))
    round_two = tuple((p[1].astype(jnp.float32) for p in params))
    nodes = node_input.astype(jnp.float32).reshape(graphs, NODES_MB, LATENT)
    edges = edge_input.astype(jnp.float32).reshape(graphs, EDGES_MB, LATENT)
    sender = senders.reshape(graphs, EDGES_MB).astype(jnp.int32)
    receiver = receivers.reshape(graphs, EDGES_MB).astype(jnp.int32)
    pad_nodes = jnp.zeros_like(nodes)
    pad_edges = jnp.zeros_like(edges)

    def forward(first, second, nodes, edges, plus_nodes, plus_edges):

        def graph(items):
            node, edge, send, recv, add_node, add_edge = items
            node_one, edge_one = one_round(first, node, edge, send, recv)
            node_one = node_one + add_node
            edge_one = edge_one + add_edge
            node_two, edge_two = one_round(second, node_one, edge_one, send, recv)
            return (node_one, edge_one, node_two, edge_two)
        return lax.map(jax.checkpoint(graph), (nodes, edges, sender, receiver, plus_nodes, plus_edges))
    outs, pull = jax.vjp(forward, round_one, round_two, nodes, edges, pad_nodes, pad_edges)
    node_one, edge_one, node_two, edge_two = outs
    cot = (jnp.zeros_like(node_one), jnp.zeros_like(edge_one), node_cot.astype(jnp.float32).reshape(graphs, NODES_MB, LATENT), edge_cot.astype(jnp.float32).reshape(graphs, EDGES_MB, LATENT))
    grad_one, grad_two, grad_nodes, grad_edges, grad_mid_nodes, grad_mid_edges = pull(cot)
    node_latents = jnp.stack([node_one, node_two]).reshape(2, NODES, LATENT)
    edge_latents = jnp.stack([edge_one, edge_two]).reshape(2, EDGES, LATENT)
    node_grads = jnp.stack([grad_nodes, grad_mid_nodes]).reshape(2, NODES, LATENT)
    edge_grads = jnp.stack([grad_edges, grad_mid_edges]).reshape(2, EDGES, LATENT)
    weight_grads = tuple((jnp.stack([a, b]) for a, b in zip(grad_one, grad_two)))
    return (node_latents, edge_latents, node_grads, edge_grads, weight_grads[0], weight_grads[1], weight_grads[2], weight_grads[3], weight_grads[4], weight_grads[5], weight_grads[6], weight_grads[7], weight_grads[8], weight_grads[9], weight_grads[10], weight_grads[11])
```

```python
import functools

import jax
import jax.numpy as jnp
from jax import lax
from jax.experimental import pallas as pl
from jax.experimental.pallas import tpu as pltpu
from jax.sharding import PartitionSpec as P

MICRO = 4
EPS = 1e-05
BLOCK = 512
F32 = jnp.float32
BF16 = jnp.bfloat16


def dot(left, right):
    return jnp.dot(left, right, preferred_element_type=F32)


def dot_tn(left, right):
    return lax.dot_general(left, right, (((0,), (0,)), ((), ())), preferred_element_type=F32)


def dot_nt(left, right):
    return lax.dot_general(left, right, (((1,), (1,)), ((), ())), preferred_element_type=F32)


def col_sum(value):
    return jnp.sum(value, axis=0, keepdims=True)


def row_mean(value):
    return jnp.mean(value, axis=1, keepdims=True)


def half_silu(half):
    t = jnp.tanh(half)
    up = 1.0 + t
    act = half * up
    return act, up + act * (1.0 - t)


def centre(w):
    w = w.astype(F32)
    return (w - row_mean(w)).astype(BF16)


def graph_kernel(
    which,
    nodes,
    edges,
    width,
    sec_ref,
    idx_s,
    idx_r,
    node_hbm,
    edge_hbm,
    ncot_hbm,
    ecot_hbm,
    w_mine,
    w_theirs,
    v_mine,
    v_theirs,
    *rest,
):
    n_prev = 6 if which > 0 else 0
    prev = rest[:n_prev]
    (lat_e, lat_n, gr_e, gr_n, send_e, send_n, wg, vg) = rest[n_prev : n_prev + 8]
    (
        sr,
        srt,
        e0,
        e1,
        cot,
        act0,
        act1,
        dd0,
        dd1,
        xh0,
        xh1,
        inv0,
        inv1,
        big,
        low,
        wv,
        hb,
        h0_in,
        cotn,
        nf,
        nlow,
        tot,
        gacc,
        pp,
        sems,
    ) = rest[n_prev + 8 :]
    acts, dds, xhs, invs = (act0, act1), (dd0, dd1), (xh0, xh1), (inv0, inv1)
    sec = sec_ref[0]
    gi = 2 * sec + which
    erow = pl.multiple_of(gi * edges, edges)
    nrow = pl.multiple_of(gi * nodes, nodes)
    first = sec == 0
    n = BLOCK
    blocks = edges // n

    def copy(src, dst, k):
        return pltpu.make_async_copy(src, dst, sems.at[k])

    loads = [
        copy(edge_hbm.at[pl.ds(erow, edges)], e0, 0),
        copy(node_hbm.at[pl.ds(nrow, nodes)], h0_in, 1),
        copy(ecot_hbm.at[pl.ds(erow, edges)], cot, 2),
        copy(ncot_hbm.at[pl.ds(nrow, nodes)], cotn, 3),
    ]
    if which > 0:
        loads += [copy(prev[4], wg, 6), copy(prev[5], vg, 7)]
    for c in loads:
        c.start()

    @pl.when(first)
    def _():
        copy(w_mine, wv.at[0], 4).start()
        copy(w_theirs, wv.at[1], 5).start()

    @pl.when(jnp.logical_not(first))
    def _():
        copy(w_theirs, wv.at[0], 4).start()
        copy(w_mine, wv.at[1], 5).start()

    rows = edges // 128
    irow = pl.multiple_of(gi * rows, rows)
    for k, idx in enumerate((idx_s, idx_r)):

        def build(j, carry, k=k, idx=idx):
            row = idx[pl.ds(irow + j, 1), :]
            at = pl.multiple_of(j * 128, 128)
            up = lax.broadcasted_iota(jnp.int32, (nodes, 128), 0)
            srt[pl.ds(k * nodes, nodes), pl.ds(at, 128)] = jnp.where(up == row, 1.0, 0.0).astype(BF16)
            column = jnp.broadcast_to(row, (128, 128)).T
            along = lax.broadcasted_iota(jnp.int32, (128, 128), 1)
            for c in range(nodes // 128):
                sr[pl.ds(at, 128), pl.ds(k * nodes + c * 128, 128)] = jnp.where(
                    along + c * 128 == column, 1.0, 0.0
                ).astype(BF16)
            return carry

        lax.fori_loop(0, rows, build, 0)

    for c in loads:
        c.wait()
    copy(w_mine, wv.at[0], 4).wait()
    copy(w_mine, wv.at[1], 5).wait()

    def vec(r, k):
        mine = v_mine[pl.ds(k, 1), :]
        theirs = v_theirs[pl.ds(k, 1), :]
        return jnp.where(first, mine, theirs) if r == 0 else jnp.where(first, theirs, mine)

    def weights(r):
        at = 0
        out = []
        for rows_of in (width, width, width, width, width, width, width):
            out.append(wv[r, at : at + rows_of, :])
            at += rows_of
        return out

    def out_copies(r, kind, start):
        full, slot = (lat_e, lat_n) if kind == 0 else (gr_e, gr_n), kind
        mine = sec == r

        def go(c):
            if start:
                c.start()
            else:
                c.wait()

        src = (e1 if r == 0 else low) if kind == 0 else (low if r == 1 else e1)

        @pl.when(mine)
        def _():
            go(copy(big, full[0].at[pl.ds(erow, edges)], 6))
            go(copy(nf, full[1].at[pl.ds(nrow, nodes)], 7))

        @pl.when(jnp.logical_not(mine))
        def _():
            go(copy(src, send_e.at[slot], 6))
            go(copy(nlow, send_n.at[slot], 7))

    saved = []

    def forward(r, e_ref, h, out_low):
        we, ws, wr, w2, w3a, w3b, w4 = weights(r)
        hl = h.astype(BF16)
        hb[r] = hl
        pp[:nodes, :] = (dot(hl, ws) * 0.5).astype(BF16)
        pp[nodes:, :] = ((dot(hl, wr) + vec(r, 0)) * 0.5).astype(BF16)
        we_h = we * 0.5
        w2c = centre(w2)
        b2 = vec(r, 1)
        b2c = b2 - row_mean(b2)
        gain, shift = vec(r, 2), vec(r, 3)
        tot[...] = jnp.zeros_like(tot)

        def body(b, carry):
            at = pl.multiple_of(b * n, n)
            here = pl.ds(at, n)
            e = e_ref[here, :]
            half = dot(e, we_h) + dot(sr[here, :], pp[...])
            act, slope = half_silu(half)
            act = act.astype(BF16)
            acts[r][here, :] = act
            dds[r][here, :] = slope.astype(BF16)
            z = dot(act, w2c) + b2c
            inv = lax.rsqrt(row_mean(z * z) + EPS)
            xh = z * inv
            xhs[r][here, :] = xh.astype(BF16)
            invs[r][here, :] = jnp.broadcast_to(inv, (n, 128))
            message = xh * gain + shift
            out = e.astype(F32) + message
            big[here, :] = out
            out_low[here, :] = out.astype(BF16)
            tot[...] += dot(srt[nodes:, here], message.astype(BF16))
            return carry

        lax.fori_loop(0, blocks, body, 0)
        tl = tot[...].astype(BF16)
        half = (dot(hl, w3a) + dot(tl, w3b) + vec(r, 4)) * 0.5
        act, slope = half_silu(half)
        act = act.astype(BF16)
        z = dot(act, centre(w4))
        b4 = vec(r, 5)
        z = z + (b4 - row_mean(b4))
        inv = lax.rsqrt(row_mean(z * z) + EPS)
        xh = z * inv
        out = h + xh * vec(r, 6) + vec(r, 7)
        nf[...] = out
        nlow[...] = out.astype(BF16)
        saved.append((hl, tl, act, slope, xh, inv))
        return out

    def backward(r, e_ref, de_ref, dn, out_low):
        we, ws, wr, w2, w3a, w3b, w4 = weights(r)
        hl, tl, act_n, slope_n, xh_n, inv_n = saved[r]
        slot = r ^ sec
        w_out = wg.at[slot]
        v_out = vg.at[slot]

        def put_w(at, value):
            if which > 0:
                value = value + w_out[at : at + value.shape[0], :]
            w_out[at : at + value.shape[0], :] = value

        def put_v(k, value):
            if which > 0:
                value = value + v_out[k : k + 1, :]
            v_out[k : k + 1, :] = value

        gain_n = vec(r, 6)
        g = dn * gain_n
        put_v(6, col_sum(dn * xh_n))
        put_v(7, col_sum(dn))
        d4 = (inv_n * (g - row_mean(g) - xh_n * row_mean(g * xh_n))).astype(BF16)
        put_w(6 * width, dot_tn(act_n, d4))
        put_v(5, col_sum(d4.astype(F32)))
        d3 = (dot_nt(d4, w4) * slope_n * 0.5).astype(BF16)
        put_w(4 * width, dot_tn(hl, d3))
        put_w(5 * width, dot_tn(tl, d3))
        put_v(4, col_sum(d3.astype(F32)))
        dh = dn + dot_nt(d3, w3a)
        dtotal = dot_nt(d3, w3b).astype(BF16)
        gain = vec(r, 2)
        w2h = w2 * 0.5
        gacc[...] = jnp.zeros_like(gacc)

        def body(b, carry):
            s_gx, s_g, s_2, dw2, dwe = carry
            at = pl.multiple_of(b * n, n)
            here = pl.ds(at, n)
            de = de_ref[here, :].astype(F32)
            xh = xhs[r][here, :].astype(F32)
            inv = invs[r][here, :1]
            g = (de + dot(sr[here, nodes:], dtotal)) * gain
            gx = g * xh
            d2 = inv * (g - row_mean(g) - xh * row_mean(gx))
            s_gx = s_gx + col_sum(gx)
            s_g = s_g + col_sum(g)
            s_2 = s_2 + col_sum(d2)
            d2 = d2.astype(BF16)
            dw2 = dw2 + dot_tn(acts[r][here, :], d2)
            d1 = (dot_nt(d2, w2h) * dds[r][here, :].astype(F32)).astype(BF16)
            dwe = dwe + dot_tn(e_ref[here, :], d1)
            gacc[...] += dot(srt[:, here], d1)
            out = de + dot_nt(d1, we)
            big[here, :] = out
            out_low[here, :] = out.astype(BF16)
            return s_gx, s_g, s_2, dw2, dwe

        row0 = jnp.zeros((1, width), F32)
        square0 = jnp.zeros((width, width), F32)
        s_gx, s_g, s_2, dw2, dwe = lax.fori_loop(0, blocks, body, (row0, row0, row0, square0, square0))
        put_v(2, s_gx / gain)
        put_v(3, s_g / gain)
        put_v(1, s_2)
        put_w(3 * width, dw2)
        put_w(0, dwe)
        put_v(0, col_sum(gacc[nodes:, :]))
        gs = gacc[:nodes, :].astype(BF16)
        gr = gacc[nodes:, :].astype(BF16)
        put_w(width, dot_tn(hl, gs))
        put_w(2 * width, dot_tn(hl, gr))
        dh = dh + dot_nt(gs, ws) + dot_nt(gr, wr)
        nf[...] = dh
        nlow[...] = dh.astype(BF16)
        return dh

    h1 = forward(0, e0, h0_in[...].astype(F32), e1)
    out_copies(0, 0, True)
    out_copies(0, 0, False)
    forward(1, e1, h1, low)
    out_copies(1, 0, True)
    out_copies(1, 0, False)
    d1 = backward(1, e1, cot, cotn[...].astype(F32), low)
    out_copies(1, 1, True)
    out_copies(1, 1, False)
    backward(0, e0, low, d1, e1)
    out_copies(0, 1, True)
    out_copies(0, 1, False)


def run_graph(which, nodes, edges, sec, idx_s, idx_r, node, edge, ncot, ecot, w_mine, w_theirs, v_mine, v_theirs, prev):
    width = node.shape[1]
    any_spec = pl.BlockSpec(memory_space=pl.ANY)
    vmem = pl.BlockSpec(memory_space=pltpu.VMEM)
    smem = pl.BlockSpec(memory_space=pltpu.SMEM)
    shape = jax.ShapeDtypeStruct
    outs = (
        shape((edge.shape[0], width), F32),
        shape((node.shape[0], width), F32),
        shape((edge.shape[0], width), F32),
        shape((node.shape[0], width), F32),
        shape((2, edges, width), BF16),
        shape((2, nodes, width), BF16),
        shape((2, w_mine.shape[0], width), F32),
        shape((2, 8, width), F32),
    )
    ins = [sec, idx_s, idx_r, node, edge, ncot, ecot, w_mine, w_theirs, v_mine, v_theirs]
    in_specs = [smem, vmem, vmem] + [any_spec] * 6 + [vmem, vmem]
    aliases = {}
    if prev is not None:
        base = len(ins)
        ins = ins + list(prev)
        in_specs = in_specs + [any_spec] * 6
        aliases = {base + i: i for i in range(4)}
    big = lambda dt: pltpu.VMEM((edges, width), dt)
    return pl.pallas_call(
        functools.partial(graph_kernel, which, nodes, edges, width),
        out_shape=outs,
        in_specs=in_specs,
        out_specs=(any_spec,) * 6 + (vmem, vmem),
        input_output_aliases=aliases,
        scratch_shapes=[
            pltpu.VMEM((edges, 2 * nodes), BF16),
            pltpu.VMEM((2 * nodes, edges), BF16),
            big(BF16),
            big(BF16),
            big(BF16),
            big(BF16),
            big(BF16),
            big(BF16),
            big(BF16),
            big(BF16),
            big(BF16),
            pltpu.VMEM((edges, 128), F32),
            pltpu.VMEM((edges, 128), F32),
            big(F32),
            big(BF16),
            pltpu.VMEM((2, w_mine.shape[0], width), BF16),
            pltpu.VMEM((2, nodes, width), BF16),
            pltpu.VMEM((nodes, width), BF16),
            pltpu.VMEM((nodes, width), BF16),
            pltpu.VMEM((nodes, width), F32),
            pltpu.VMEM((nodes, width), BF16),
            pltpu.VMEM((nodes, width), F32),
            pltpu.VMEM((2 * nodes, width), F32),
            pltpu.VMEM((2 * nodes, width), BF16),
            pltpu.SemaphoreType.DMA((8,)),
        ],
        compiler_params=pltpu.CompilerParams(vmem_limit_bytes=60 * 2**20),
        name=f"graph_{which}",
    )(*ins)


def spread_kernel(sec_ref, recv_ref, full_ref, out_ref):
    out_ref[...] = recv_ref[...].astype(F32)


def spread(full, recv, sec, graph, kind, rows):
    width = full.shape[1]
    steps = recv.shape[1] // rows

    def place(i, sec_ref):
        return ((2 * (1 - sec_ref[0]) + graph) * steps + i, 0)

    return pl.pallas_call(
        spread_kernel,
        grid_spec=pltpu.PrefetchScalarGridSpec(
            num_scalar_prefetch=1,
            grid=(steps,),
            in_specs=[
                pl.BlockSpec((None, rows, width), lambda i, sec_ref: (kind, i, 0)),
                pl.BlockSpec(memory_space=pl.ANY),
            ],
            out_specs=pl.BlockSpec((rows, width), place),
        ),
        out_shape=jax.ShapeDtypeStruct(full.shape, F32),
        input_output_aliases={2: 0},
        name="spread",
    )(sec, recv, full)


def reduce_over_dp(value):
    devices = lax.axis_size("dp")
    sec = lax.axis_index("section")
    me = lax.axis_index("dp")
    bits = [1 << k for k in range(devices.bit_length() - 1)]
    orders = [bits, bits[:2][::-1] + bits[2:]]
    halved = min(2, len(bits))

    def swap(part, step):
        pairs = [
            (s * devices + i, s * devices + (i ^ orders[s][step]))
            for s in range(2)
            for i in range(devices)
        ]
        return lax.ppermute(part, ("section", "dp"), pairs)

    def high(step):
        return jnp.where(sec == 0, me // orders[0][step], me // orders[1][step]) % 2

    part = value
    for step in range(halved):
        half = part.shape[0] // 2
        mine = high(step)
        keep = lax.dynamic_slice_in_dim(part, mine * half, half, 0)
        send = lax.dynamic_slice_in_dim(part, (1 - mine) * half, half, 0)
        got = swap(send.astype(BF16), step)
        part = keep.astype(F32) + got.astype(F32)
    for step in range(halved, len(bits)):
        part = part + swap(part.astype(BF16), step).astype(F32)
    for step in reversed(range(halved)):
        got = swap(part.astype(BF16), step).astype(F32)
        part = jnp.where(
            high(step) == 0, jnp.concatenate([part, got], 0), jnp.concatenate([got, part], 0)
        )
    return part


def shards(
    node_input,
    edge_input,
    senders,
    receivers,
    node_cot,
    edge_cot,
    edge_w1,
    edge_b1,
    edge_w2,
    edge_b2,
    edge_gain,
    edge_shift,
    node_w1,
    node_b1,
    node_w2,
    node_b2,
    node_gain,
    node_shift,
):
    nodes = node_input.shape[0] // MICRO
    edges = edge_input.shape[0] // MICRO
    width = node_input.shape[1]
    sec = lax.axis_index("section").reshape(1).astype(jnp.int32)
    other = [(0, 1), (1, 0)]
    w_mine = jnp.concatenate([edge_w1[0], edge_w2[0], node_w1[0], node_w2[0]], axis=0)
    v_mine = jnp.concatenate(
        [edge_b1, edge_b2, edge_gain, edge_shift, node_b1, node_b2, node_gain, node_shift], axis=0
    )
    w_theirs = lax.ppermute(w_mine, "section", other)
    v_theirs = lax.ppermute(v_mine, "section", other)
    idx_s = senders.reshape(-1, 128)
    idx_r = receivers.reshape(-1, 128)
    prev = None
    got = []
    for which in range(2):
        out = run_graph(
            which,
            nodes,
            edges,
            sec,
            idx_s,
            idx_r,
            node_input,
            edge_input,
            node_cot,
            edge_cot,
            w_mine,
            w_theirs,
            v_mine,
            v_theirs,
            prev,
        )
        got.append((lax.ppermute(out[4], "section", other), lax.ppermute(out[5], "section", other)))
        prev = (out[0], out[1], out[2], out[3], out[6], out[7])
    wg, vg = prev[4], prev[5]
    both = jnp.concatenate([wg, vg], axis=1)
    mine = both[0] + lax.ppermute(both[1].astype(BF16), "section", other).astype(F32)
    total = reduce_over_dp(mine)
    lat_e, lat_n, gr_e, gr_n = prev[:4]
    for which in range(2):
        recv_e, recv_n = got[which]
        lat_e = spread(lat_e, recv_e, sec, which, 0, 1024)
        gr_e = spread(gr_e, recv_e, sec, which, 1, 1024)
        lat_n = spread(lat_n, recv_n, sec, which, 0, nodes)
        gr_n = spread(gr_n, recv_n, sec, which, 1, nodes)
    w1, w2, n1, n2 = 3 * width, 4 * width, 6 * width, 7 * width
    vecs = [total[n2 + k][None] for k in range(8)]
    return (
        lat_n[None],
        lat_e[None],
        gr_n[None],
        gr_e[None],
        total[:w1][None],
        vecs[0],
        total[w1:w2][None],
        vecs[1],
        vecs[2],
        vecs[3],
        total[w2:n1][None],
        vecs[4],
        total[n1:n2][None],
        vecs[5],
        vecs[6],
        vecs[7],
    )


def solution(mesh):
    rows = P("dp", None)
    mat = P("section", None, None)
    row = P("section", None)
    in_specs = (rows, rows, P("dp"), P("dp"), rows, rows) + (mat, row, mat, row, row, row) * 2
    whole = P("section", "dp", None)
    out_specs = (whole,) * 4 + (mat, row, mat, row, row, row) * 2
    return jax.shard_map(shards, mesh=mesh, in_specs=in_specs, out_specs=out_specs, check_vma=False)
```

```python
import functools

import jax
import jax.numpy as jnp
from jax import lax
from jax.experimental import pallas as pl
from jax.experimental.pallas import tpu as pltpu
from jax.sharding import PartitionSpec as P

MICRO = 4
EPS = 1e-05
BLOCK = 256
CHUNK = 1024
GRAD_ROWS = 1856
F32 = jnp.float32
BF16 = jnp.bfloat16


def dot(left, right):
    return jnp.dot(left, right, preferred_element_type=F32)


def dot_tn(left, right):
    return lax.dot_general(left, right, (((0,), (0,)), ((), ())), preferred_element_type=F32)


def dot_nt(left, right):
    return lax.dot_general(left, right, (((1,), (1,)), ((), ())), preferred_element_type=F32)


def col_sum(value):
    return jnp.sum(value, axis=0, keepdims=True)


def row_mean(value):
    return jnp.mean(value, axis=1, keepdims=True)


def half_silu(half):
    t = jnp.tanh(half)
    up = 1.0 + t
    act = half * up
    return act, up + act * (1.0 - t)


def centre(w):
    w = w.astype(F32)
    return (w - row_mean(w)).astype(BF16)


def interleave(parts, skew):
    parts = list(parts)
    done = [False] * len(parts)
    clock = 0
    while not all(done):
        for i, part in enumerate(parts):
            if clock >= i * skew and not done[i]:
                done[i] = next(part, "end") == "end"
        clock += 1


def graph_kernel(
    which,
    nodes,
    edges,
    width,
    sec_ref,
    idx_s,
    idx_r,
    node_hbm,
    edge_hbm,
    ncot_hbm,
    ecot_hbm,
    w_mine,
    w_theirs,
    v_mine,
    v_theirs,
    *rest,
):
    n_prev = 4 if which > 0 else 0
    (lat_e, lat_n, gr_e, gr_n, send_e, send_n, wg_keep, wg_send) = rest[n_prev : n_prev + 8]
    (
        es,
        srt,
        cot,
        low,
        act0,
        act1,
        dd0,
        dd1,
        xh0,
        xh1,
        inv0,
        inv1,
        big,
        wv,
        h0_in,
        cotn,
        nf,
        nlow,
        tot,
        gacc,
        dh_own,
        pw,
        jn,
        act_n,
        slope_n,
        xh_n,
        inv_n,
        wg,
        wl,
        load_sems,
        big_sem,
        send_sems,
        node_sems,
        grad_sems,
    ) = rest[n_prev + 8 :]
    acts, dds, xhs, invs = (act0, act1), (dd0, dd1), (xh0, xh1), (inv0, inv1)
    sec = sec_ref[0]
    gi = 2 * sec + which
    erow = pl.multiple_of(gi * edges, edges)
    nrow = pl.multiple_of(gi * nodes, nodes)
    first = sec == 0
    n = BLOCK
    col_s, col_r, col_1 = width, width + nodes, width + 2 * nodes
    spans = (slice(0, col_1), slice(col_s, col_1 + width))
    own = (slice(0, width), slice(col_1, col_1 + width))
    copy = pltpu.make_async_copy

    loads = [
        copy(edge_hbm.at[pl.ds(erow, edges)], es.at[:, own[0]], load_sems.at[0]),
        copy(node_hbm.at[pl.ds(nrow, nodes)], h0_in, load_sems.at[1]),
    ]
    late = [
        copy(ecot_hbm.at[pl.ds(erow, edges)], cot, load_sems.at[2]),
        copy(ncot_hbm.at[pl.ds(nrow, nodes)], cotn, load_sems.at[3]),
    ]
    other_row = pl.multiple_of((2 * (1 - sec) + which) * edges, edges)
    for c in loads:
        c.start()

    @pl.when(first)
    def _():
        copy(w_mine, wv.at[0], load_sems.at[4]).start()
        copy(w_theirs, wv.at[1], load_sems.at[5]).start()

    @pl.when(jnp.logical_not(first))
    def _():
        copy(w_theirs, wv.at[0], load_sems.at[4]).start()
        copy(w_mine, wv.at[1], load_sems.at[5]).start()

    rows = edges // 128
    irow = pl.multiple_of(gi * rows, rows)

    def build(j, carry):
        at = pl.multiple_of(j * 128, 128)
        for k, idx in enumerate((idx_s, idx_r)):
            row = idx[pl.ds(irow + j, 1), :]
            up = lax.broadcasted_iota(jnp.int32, (nodes, 128), 0)
            srt[pl.ds(k * nodes, nodes), pl.ds(at, 128)] = jnp.where(up == row, 1.0, 0.0).astype(BF16)
            column = jnp.broadcast_to(row, (128, 128)).T
            along = lax.broadcasted_iota(jnp.int32, (128, 128), 1)
            for c in range(nodes // 128):
                es[pl.ds(at, 128), pl.ds(col_s + k * nodes + c * 128, 128)] = jnp.where(
                    along + c * 128 == column, 1.0, 0.0
                ).astype(BF16)
        return carry

    lax.fori_loop(0, rows, build, 0)
    wg[7 * width + 8 :, :] = jnp.zeros((wg.shape[0] - 7 * width - 8, width), F32)
    for c in loads:
        c.wait()
    copy(w_mine, wv.at[0], load_sems.at[4]).wait()
    copy(w_mine, wv.at[1], load_sems.at[5]).wait()

    def vec(r, k):
        mine = v_mine[pl.ds(k, 1), :]
        theirs = v_theirs[pl.ds(k, 1), :]
        return jnp.where(first, mine, theirs) if r == 0 else jnp.where(first, theirs, mine)

    def weights(r):
        w1 = [wv[r, k * width : (k + 1) * width, :] for k in range(3)]
        at = 3 * width
        return (
            w1[0],
            jnp.concatenate(w1[1:], axis=1),
            wv[r, at : at + width, :],
            wv[r, at + width : at + 3 * width, :],
            wv[r, at + 3 * width : at + 4 * width, :],
        )

    rounds = (0, 1, 1, 0)
    full = ((lat_e, lat_n), (lat_e, lat_n), (gr_e, gr_n), (gr_e, gr_n))
    lows = (es.at[:, own[1]], low, low, cot)

    def big_copy(phase):
        at = jnp.where(sec == rounds[phase], erow, other_row)
        at = pl.multiple_of(at, edges)
        return copy(big, full[phase][0].at[pl.ds(at, edges)], big_sem.at[0])

    def send_copies(phase):
        kind = phase // 2
        return (
            copy(lows[phase], send_e.at[kind], send_sems.at[phase]),
            copy(nlow.at[phase % 2], send_n.at[kind], node_sems.at[phase]),
        )

    def node_copy(phase):
        return copy(nf.at[phase % 2], full[phase][1].at[pl.ds(nrow, nodes)], node_sems.at[phase])

    def phase_out(phase):
        @pl.when(sec == rounds[phase])
        def _():
            node_copy(phase).start()

        @pl.when(sec != rounds[phase])
        def _():
            for c in send_copies(phase):
                c.start()

    def phase_wait_edges(phase):
        @pl.when(sec != rounds[phase])
        def _():
            send_copies(phase)[0].wait()

    def phase_wait_nodes(phase):
        @pl.when(sec == rounds[phase])
        def _():
            node_copy(phase).wait()

        @pl.when(sec != rounds[phase])
        def _():
            send_copies(phase)[1].wait()

    half_n = nodes // 2

    def forward(r, h):
        phase = r
        we, wsr, w2, w3, w4 = weights(r)
        hl = h.astype(BF16)
        jn[r, :, :width] = hl
        k_e, k_s = (0, width) if r == 0 else (2 * nodes, 0)
        pw[k_e : k_e + width, :] = we * 0.5
        table = dot(hl, wsr) * 0.5
        pw[k_s : k_s + nodes, :] = table[:, :width].astype(BF16)
        pw[k_s + nodes : k_s + 2 * nodes, :] = (table[:, width:] + vec(r, 0) * 0.5).astype(BF16)
        w2c = centre(w2)
        b2 = vec(r, 1)
        b2c = b2 - row_mean(b2)
        gain, shift = vec(r, 2), vec(r, 3)
        lo = lows[phase]
        message = (act1, cot)[r]
        if phase > 0:
            big_copy(phase - 1).wait()

        def block(i):
            here = slice(i * n, (i + 1) * n)
            half = dot(es[here, spans[r]], pw[...])
            yield
            act, slope = half_silu(half)
            act = act.astype(BF16)
            acts[r][here, :] = act
            dds[r][here, :] = slope.astype(BF16)
            yield
            z = dot(act, w2c)
            yield
            z = z + b2c
            inv = lax.rsqrt(row_mean(z * z) + EPS)
            xh = z * inv
            xhs[r][here, :] = xh.astype(BF16)
            invs[r][here, :] = jnp.broadcast_to(inv, (n, 128)).astype(BF16)
            update = xh * gain + shift
            message[here, :] = update.astype(BF16)
            out = es[here, own[r]].astype(F32) + update
            big[here, :] = out
            lo[here, :] = out.astype(BF16)
            yield
            if (i + 1) * n % CHUNK == 0:
                part = slice((i + 1) * n - CHUNK, (i + 1) * n)
                add = dot(srt[nodes:, part], message[part, :])
                tot[...] = add if part.start == 0 else tot[...] + add
                yield

        interleave([block(i) for i in range(edges // n)], 1)
        big_copy(phase).start()
        if r == 1:
            for c in late:
                c.start()
        w4c = centre(w4)
        b4 = vec(r, 5)
        b4c = b4 - row_mean(b4)
        b3 = vec(r, 4)

        def node_block(i):
            here = slice(i * half_n, (i + 1) * half_n)
            jn[r, here, width:] = tot[here, :].astype(BF16)
            z = dot(jn[r, here, :], w3)
            yield
            act, slope = half_silu((z + b3) * 0.5)
            act = act.astype(BF16)
            act_n[r, here, :] = act
            slope_n[r, here, :] = slope.astype(BF16)
            z = dot(act, w4c)
            yield
            z = z + b4c
            inv = lax.rsqrt(row_mean(z * z) + EPS)
            xh = z * inv
            xh_n[r, here, :] = xh.astype(BF16)
            inv_n[r, here, :] = jnp.broadcast_to(inv, (half_n, 128))
            h_here = h[here, :] if r == 0 else nf[0, here, :]
            out = h_here + xh * vec(r, 6) + vec(r, 7)
            nf[phase % 2, here, :] = out
            nlow[phase % 2, here, :] = out.astype(BF16)
            yield

        interleave([node_block(i) for i in range(2)], 1)
        phase_out(phase)
        return nf[phase % 2]

    def backward(r, de_ref, dn):
        phase = 3 - r
        we, wsr, w2, w3, w4 = weights(r)

        if r == 0:

            @pl.when(sec == 1)
            def _():
                copy(wg, wg_keep, grad_sems.at[0]).wait()

        def put_w(at, value):
            wg[at : at + value.shape[0], :] = value

        def put_v(k, value):
            put_w(7 * width + k, value)

        gain_n = vec(r, 6)
        d4s, d3s, djs = {}, {}, {}

        def node_block(i):
            here = slice(i * half_n, (i + 1) * half_n)
            xh = xh_n[r, here, :].astype(F32)
            g = dn[here, :] * gain_n
            d4 = inv_n[r, here, :1] * (g - row_mean(g) - xh * row_mean(g * xh))
            d4s[i] = d4.astype(BF16)
            d3 = dot_nt(d4s[i], w4)
            yield
            d3s[i] = (d3 * slope_n[r, here, :].astype(F32) * 0.5).astype(BF16)
            djs[i] = dot_nt(d3s[i], w3)
            yield

        interleave([node_block(i) for i in range(2)], 1)
        djn = jnp.concatenate([djs[0], djs[1]], axis=0)
        dtotal = djn[:, width:].astype(BF16)
        dh_own[...] = djn[:, :width]
        d4 = jnp.concatenate([d4s[0], d4s[1]], axis=0)
        d3 = jnp.concatenate([d3s[0], d3s[1]], axis=0)
        put_w(6 * width, dot_tn(act_n[r], d4))
        put_w(4 * width, dot_tn(jn[r], d3))
        put_v(6, col_sum(dn * xh_n[r].astype(F32)))
        put_v(7, col_sum(dn))
        put_v(5, col_sum(d4.astype(F32)))
        put_v(4, col_sum(d3.astype(F32)))
        gain = vec(r, 2)
        w2h = w2 * 0.5
        lo = lows[phase]
        sums = [jnp.zeros((1, width), F32)] * 3
        squares = [None, None]
        big_copy(phase - 1).wait()

        def block(i):
            here = slice(i * n, (i + 1) * n)
            g = dot(es[here, col_r:col_1], dtotal)
            yield
            xh = xhs[r][here, :].astype(F32)
            inv = invs[r][here, :1].astype(F32)
            g = (de_ref[here, :].astype(F32) + g) * gain
            gx = g * xh
            d2 = inv * (g - row_mean(g) - xh * row_mean(gx))
            for k, value in enumerate((gx, g, d2)):
                sums[k] = sums[k] + col_sum(value)
            d2 = d2.astype(BF16)
            xhs[r][here, :] = d2
            yield
            d1 = dot_nt(d2, w2h)
            yield
            d1 = (d1 * dds[r][here, :].astype(F32)).astype(BF16)
            dds[r][here, :] = d1
            yield
            back = dot_nt(d1, we)
            yield
            out = de_ref[here, :].astype(F32) + back
            big[here, :] = out
            lo[here, :] = out.astype(BF16)
            yield
            if (i + 1) * n % CHUNK == 0:
                part = slice((i + 1) * n - CHUNK, (i + 1) * n)
                add = dot(srt[:, part], dds[r][part, :])
                gacc[...] = add if part.start == 0 else gacc[...] + add
                yield

        interleave([block(i) for i in range(edges // n)], 1)
        big_copy(phase).start()
        dw2 = dot_tn(acts[r][...], xhs[r][...])
        dwe = dot_tn(es[:, own[r]], dds[r][...])
        s_gx, s_g, s_2 = sums
        put_v(2, s_gx / gain)
        put_v(3, s_g / gain)
        put_v(1, s_2)
        put_w(3 * width, dw2)
        put_w(0, dwe)
        put_v(0, col_sum(gacc[nodes:, :]))
        both = jnp.concatenate([gacc[:nodes, :], gacc[nodes:, :]], axis=1).astype(BF16)
        out = dn + dh_own[...] + dot_nt(both, wsr)
        phase_wait_nodes(phase - 2)
        nf[phase % 2] = out
        nlow[phase % 2] = out.astype(BF16)
        phase_out(phase)
        dws = dot_tn(jn[r, :, :width], both)
        put_w(width, dws[:, :width])
        put_w(2 * width, dws[:, width:])

        @pl.when(sec == r)
        def _():
            copy(wg, wg_keep, grad_sems.at[0]).start()

        @pl.when(sec != r)
        def _():
            wl[...] = wg[...].astype(BF16)
            copy(wl, wg_send, grad_sems.at[1]).start()

        return nf[phase % 2]

    h1 = forward(0, h0_in[...].astype(F32))
    forward(1, h1)
    for c in late:
        c.wait()
    phase_wait_edges(1)
    d1 = backward(1, cot, cotn[...].astype(F32))
    backward(0, low, d1)
    for phase in (0, 2, 3):
        phase_wait_edges(phase)
    for phase in (2, 3):
        phase_wait_nodes(phase)

    @pl.when(sec == 0)
    def _():
        copy(wg, wg_keep, grad_sems.at[0]).wait()

    copy(wl, wg_send, grad_sems.at[1]).wait()
    big_copy(3).wait()


def run_graph(which, nodes, edges, sec, idx_s, idx_r, node, edge, ncot, ecot, w_mine, w_theirs, v_mine, v_theirs, prev):
    width = node.shape[1]
    any_spec = pl.BlockSpec(memory_space=pl.ANY)
    vmem = pl.BlockSpec(memory_space=pltpu.VMEM)
    smem = pl.BlockSpec(memory_space=pltpu.SMEM)
    shape = jax.ShapeDtypeStruct
    outs = (
        shape((edge.shape[0], width), F32),
        shape((node.shape[0], width), F32),
        shape((edge.shape[0], width), F32),
        shape((node.shape[0], width), F32),
        shape((2, edges, width), BF16),
        shape((2, nodes, width), BF16),
        shape((GRAD_ROWS, width), F32),
        shape((GRAD_ROWS, width), BF16),
    )
    ins = [sec, idx_s, idx_r, node, edge, ncot, ecot, w_mine, w_theirs, v_mine, v_theirs]
    in_specs = [smem, vmem, vmem] + [any_spec] * 6 + [vmem, vmem]
    aliases = {}
    if prev is not None:
        base = len(ins)
        ins = ins + list(prev)
        in_specs = in_specs + [any_spec] * 4
        aliases = {base + i: i for i in range(4)}
    return pl.pallas_call(
        functools.partial(graph_kernel, which, nodes, edges, width),
        out_shape=outs,
        in_specs=in_specs,
        out_specs=(any_spec,) * 8,
        input_output_aliases=aliases,
        scratch_shapes=[
            pltpu.VMEM((edges, 2 * width + 2 * nodes), BF16),
            pltpu.VMEM((2 * nodes, edges), BF16),
            *[pltpu.VMEM((edges, width), BF16)] * 8,
            *[pltpu.VMEM((edges, 128), BF16)] * 2,
            pltpu.VMEM((edges, width), F32),
            pltpu.VMEM((2, w_mine.shape[0], width), BF16),
            pltpu.VMEM((nodes, width), BF16),
            pltpu.VMEM((nodes, width), BF16),
            pltpu.VMEM((2, nodes, width), F32),
            pltpu.VMEM((2, nodes, width), BF16),
            pltpu.VMEM((nodes, width), F32),
            pltpu.VMEM((2 * nodes, width), F32),
            pltpu.VMEM((nodes, width), F32),
            pltpu.VMEM((2 * nodes + width, width), BF16),
            pltpu.VMEM((2, nodes, 2 * width), BF16),
            *[pltpu.VMEM((2, nodes, width), BF16)] * 3,
            pltpu.VMEM((2, nodes, 128), F32),
            pltpu.VMEM((GRAD_ROWS, width), F32),
            pltpu.VMEM((GRAD_ROWS, width), BF16),
            pltpu.SemaphoreType.DMA((8,)),
            pltpu.SemaphoreType.DMA((1,)),
            pltpu.SemaphoreType.DMA((4,)),
            pltpu.SemaphoreType.DMA((4,)),
            pltpu.SemaphoreType.DMA((2,)),
        ],
        compiler_params=pltpu.CompilerParams(vmem_limit_bytes=60 * 2**20),
        cost_estimate=pl.CostEstimate(flops=40 * 2 * edges * width * width, transcendentals=0, bytes_accessed=2**24),
        name=f"graph_{which}",
    )(*ins)


def spread_kernel(which, nodes, edges, rows, sec_ref, recv_e, recv_n, *rest):
    outs = rest[4:8]
    e_in, n_in, e_out, n_out, in_sems, out_sems = rest[8:]
    graph = 2 * (1 - sec_ref[0]) + which
    parts = []
    for kind in range(2):
        at = pl.multiple_of(graph * nodes, nodes)
        parts.append((recv_n.at[kind], n_in.at[kind], n_out.at[kind], outs[2 * kind + 1].at[pl.ds(at, nodes)]))
        for i in range(edges // rows):
            here = pl.ds(i * rows, rows)
            at = pl.multiple_of(graph * edges + i * rows, rows)
            there = outs[2 * kind].at[pl.ds(at, rows)]
            parts.append((recv_e.at[kind, here], e_in.at[kind, here], e_out.at[kind, here], there))
    reads = [pltpu.make_async_copy(p[0], p[1], in_sems.at[i]) for i, p in enumerate(parts)]
    writes = [pltpu.make_async_copy(p[2], p[3], out_sems.at[i]) for i, p in enumerate(parts)]
    for c in reads:
        c.start()
    for p, r, w in zip(parts, reads, writes):
        r.wait()
        p[2][...] = p[1][...].astype(F32)
        w.start()
    for w in writes:
        w.wait()


def spread(which, nodes, edges, sec, recv_e, recv_n, full):
    width = recv_e.shape[2]
    rows = 1024
    count = 2 * (edges // rows + 1)
    any_spec = pl.BlockSpec(memory_space=pl.ANY)
    return pl.pallas_call(
        functools.partial(spread_kernel, which, nodes, edges, rows),
        out_shape=tuple(jax.ShapeDtypeStruct(f.shape, f.dtype) for f in full),
        in_specs=[pl.BlockSpec(memory_space=pltpu.SMEM)] + [any_spec] * 6,
        out_specs=(any_spec,) * 4,
        input_output_aliases={3 + i: i for i in range(4)},
        scratch_shapes=[
            pltpu.VMEM((2, edges, width), BF16),
            pltpu.VMEM((2, nodes, width), BF16),
            pltpu.VMEM((2, edges, width), F32),
            pltpu.VMEM((2, nodes, width), F32),
            pltpu.SemaphoreType.DMA((count,)),
            pltpu.SemaphoreType.DMA((count,)),
        ],
        compiler_params=pltpu.CompilerParams(vmem_limit_bytes=24 * 2**20),
        cost_estimate=pl.CostEstimate(flops=0, transcendentals=0, bytes_accessed=12 * (edges + nodes) * width),
        name=f"spread_{which}",
    )(sec, recv_e, recv_n, *full)


def reduce_over_dp(value, beside):
    devices = lax.axis_size("dp")
    sec = lax.axis_index("section")
    me = lax.axis_index("dp")
    bits = [1 << k for k in range(devices.bit_length() - 1)]
    orders = [bits, bits[:2][::-1] + bits[2:]]
    halved = min(2, len(bits))
    count = [0]

    def swap(part, step):
        pairs = [
            (s * devices + i, s * devices + (i ^ orders[s][step]))
            for s in range(2)
            for i in range(devices)
        ]
        part = part.astype(BF16)
        got = lax.ppermute(part, ("section", "dp"), pairs)
        if count[0] in beside:
            got = beside[count[0]](part, got)
        count[0] += 1
        return got.astype(F32)

    def high(step):
        return jnp.where(sec == 0, me // orders[0][step], me // orders[1][step]) % 2

    part = value
    for step in range(halved):
        half = part.shape[0] // 2
        mine = high(step)
        keep = lax.dynamic_slice_in_dim(part, mine * half, half, 0)
        send = lax.dynamic_slice_in_dim(part, (1 - mine) * half, half, 0)
        part = keep + swap(send, step)
    for step in range(halved, len(bits)):
        part = part + swap(part, step)
    for step in reversed(range(halved)):
        got = swap(part, step)
        if step == 0:
            return part, got, high(0)
        part = jnp.where(
            high(step) == 0, jnp.concatenate([part, got], 0), jnp.concatenate([got, part], 0)
        )
    return part[: value.shape[0] // 2], part[value.shape[0] // 2 :], jnp.zeros((), jnp.int32)


def place_kernel(flag_ref, part_ref, got_ref, *outs):
    own = flag_ref[0] == 0
    rows = part_ref.shape[0]
    at = 0
    for out in outs:
        end = at + out.shape[0]
        if at < rows:
            stop = min(end, rows)
            out[: stop - at, :] = jnp.where(own, part_ref[at:stop, :], got_ref[at:stop, :])
        if end > rows:
            start = max(at, rows)
            here = slice(start - rows, end - rows)
            out[start - at :, :] = jnp.where(own, got_ref[here, :], part_ref[here, :])
        at = end


def place(part, got, flag, sizes):
    vmem = pl.BlockSpec(memory_space=pltpu.VMEM)
    return pl.pallas_call(
        place_kernel,
        out_shape=tuple(jax.ShapeDtypeStruct((rows, part.shape[1]), F32) for rows in sizes),
        in_specs=[pl.BlockSpec(memory_space=pltpu.SMEM), vmem, vmem],
        out_specs=(vmem,) * len(sizes),
        compiler_params=pltpu.CompilerParams(vmem_limit_bytes=16 * 2**20),
        name="place",
    )(flag.reshape(1).astype(jnp.int32), part, got)


def shards(
    node_input,
    edge_input,
    senders,
    receivers,
    node_cot,
    edge_cot,
    edge_w1,
    edge_b1,
    edge_w2,
    edge_b2,
    edge_gain,
    edge_shift,
    node_w1,
    node_b1,
    node_w2,
    node_b2,
    node_gain,
    node_shift,
):
    nodes = node_input.shape[0] // MICRO
    edges = edge_input.shape[0] // MICRO
    width = node_input.shape[1]
    sec = lax.axis_index("section").reshape(1).astype(jnp.int32)
    other = [(0, 1), (1, 0)]
    w_mine = jnp.concatenate([edge_w1[0], edge_w2[0], node_w1[0], node_w2[0]], axis=0)
    v_mine = jnp.concatenate(
        [edge_b1, edge_b2, edge_gain, edge_shift, node_b1, node_b2, node_gain, node_shift], axis=0
    )
    w_theirs = lax.ppermute(w_mine, "section", other)
    v_theirs = lax.ppermute(v_mine, "section", other)
    idx_s = senders.reshape(-1, 128)
    idx_r = receivers.reshape(-1, 128)
    prev = None
    got = []
    sums = []
    for which in range(2):
        out = run_graph(
            which,
            nodes,
            edges,
            sec,
            idx_s,
            idx_r,
            node_input,
            edge_input,
            node_cot,
            edge_cot,
            w_mine,
            w_theirs,
            v_mine,
            v_theirs,
            prev,
        )
        prev = out[:4]
        sums.append((out[6], lax.ppermute(out[7], "section", other)))
        sent = out[4:6]
        if which == 1:
            mine = sum(s[0] + s[1].astype(F32) for s in sums)
            sent, mine = lax.optimization_barrier((sent, mine))
        got.append(tuple(lax.ppermute(x, "section", other) for x in sent))
    full = [prev]

    def fill(which):
        def run(sent, came):
            sent, recv, whole = lax.optimization_barrier((sent, got[which], tuple(full[0])))
            full[0] = spread(which, nodes, edges, sec, *recv, whole)
            came, full[0] = lax.optimization_barrier((came, full[0]))
            return came

        return run

    total = reduce_over_dp(mine, {0: fill(0), 3: fill(1)})
    lat_e, lat_n, gr_e, gr_n = full[0]
    out = place(*total, (3 * width, width, 2 * width, width) + (1,) * 8)
    w1, w2, n1, n2 = (w[None] for w in out[:4])
    return (
        lat_n[None],
        lat_e[None],
        gr_n[None],
        gr_e[None],
        w1,
        out[4],
        w2,
        out[5],
        out[6],
        out[7],
        n1,
        out[8],
        n2,
        out[9],
        out[10],
        out[11],
    )


def solution(mesh):
    rows = P("dp", None)
    mat = P("section", None, None)
    row = P("section", None)
    in_specs = (rows, rows, P("dp"), P("dp"), rows, rows) + (mat, row, mat, row, row, row) * 2
    whole = P("section", "dp", None)
    out_specs = (whole,) * 4 + (mat, row, mat, row, row, row) * 2
    return jax.shard_map(shards, mesh=mesh, in_specs=in_specs, out_specs=out_specs, check_vma=False)
```

```python
import functools

import jax
import jax.numpy as jnp
from jax import lax
from jax.experimental import pallas as pl
from jax.experimental.pallas import tpu as pltpu
from jax.sharding import PartitionSpec as P

MICRO = 4
GRAPHS = 2
EPS = 1e-05
BLOCK = 256
CHUNK = 1024
GRAD_ROWS = 1856
F32 = jnp.float32
BF16 = jnp.bfloat16


def dot(left, right):
    return jnp.dot(left, right, preferred_element_type=F32)


def dot_tn(left, right):
    return lax.dot_general(left, right, (((0,), (0,)), ((), ())), preferred_element_type=F32)


def dot_nt(left, right):
    return lax.dot_general(left, right, (((1,), (1,)), ((), ())), preferred_element_type=F32)


def col_sum(value):
    return jnp.sum(value, axis=0, keepdims=True)


def row_mean(value):
    return jnp.mean(value, axis=1, keepdims=True)


def half_silu(half):
    t = jnp.tanh(half)
    up = 1.0 + t
    act = half * up
    return act, up + act * (1.0 - t)


def centre(w):
    w = w.astype(F32)
    return (w - row_mean(w)).astype(BF16)


def interleave(parts, skew):
    parts = list(parts)
    done = [False] * len(parts)
    clock = 0
    while not all(done):
        for i, part in enumerate(parts):
            if clock >= i * skew and not done[i]:
                done[i] = next(part, "end") == "end"
        clock += 1


def graphs_kernel(
    nodes,
    edges,
    width,
    sec_ref,
    idx_s,
    idx_r,
    node_hbm,
    edge_hbm,
    ncot_hbm,
    ecot_hbm,
    w_mine,
    w_theirs,
    v_mine,
    v_theirs,
    lat_e,
    lat_n,
    gr_e,
    gr_n,
    send_e,
    send_n,
    wg_keep,
    wg_send,
    es,
    srt,
    cot,
    low,
    act0,
    act1,
    dd0,
    dd1,
    xh0,
    xh1,
    inv_e,
    big,
    wv,
    wc,
    vs,
    h0_in,
    cotn,
    nf,
    nlow,
    acc,
    dh_own,
    pw,
    jn,
    act_n,
    slope_n,
    xh_n,
    inv_n,
    wg,
    load_sems,
    big_sem,
    node_sems,
    low_sems,
    nlow_sems,
    grad_sems,
):
    acts, dds, xhs = (act0, act1), (dd0, dd1), (xh0, xh1)
    sec = sec_ref[0]
    first = sec == 0
    n = BLOCK
    half_n = nodes // 2
    col_s, col_r, col_1 = width, width + nodes, width + 2 * nodes
    spans = (slice(0, col_1), slice(col_s, col_1 + width))
    own = (slice(0, width), slice(col_1, col_1 + width))
    lanes = (slice(0, 64), slice(64, 128))
    copy = pltpu.make_async_copy
    rounds = (0, 1, 1, 0)
    full = ((lat_e, lat_n), (lat_e, lat_n), (gr_e, gr_n), (gr_e, gr_n))
    lows = (es.at[:, own[1]], low, low, cot)

    @pl.when(first)
    def _():
        copy(w_mine, wv.at[0], load_sems.at[4]).start()
        copy(w_theirs, wv.at[1], load_sems.at[5]).start()

    @pl.when(jnp.logical_not(first))
    def _():
        copy(w_theirs, wv.at[0], load_sems.at[4]).start()
        copy(w_mine, wv.at[1], load_sems.at[5]).start()

    vs[0] = jnp.where(first, v_mine[...], v_theirs[...])
    vs[1] = jnp.where(first, v_theirs[...], v_mine[...])
    wg[...] = jnp.zeros_like(wg)

    def vec(r, k):
        return vs[r, k : k + 1, :]

    def weights(r):
        w1 = [wv[r, k * width : (k + 1) * width, :] for k in range(3)]
        at = 3 * width
        return (
            w1[0],
            jnp.concatenate(w1[1:], axis=1),
            wv[r, at : at + width, :],
            wv[r, at + width : at + 3 * width, :],
            wv[r, at + 3 * width : at + 4 * width, :],
        )

    def put_w(r, at, value):
        here = slice(at, at + value.shape[0])
        wg[r, here, :] = wg[r, here, :] + value

    def put_v(r, k, value):
        put_w(r, 7 * width + k, value)

    def graph(which, carry):
        gi = 2 * sec + which
        other = 2 * (1 - sec) + which
        erow = pl.multiple_of(gi * edges, edges)
        nrow = pl.multiple_of(gi * nodes, nodes)

        def big_copy(phase):
            at = pl.multiple_of(jnp.where(sec == rounds[phase], gi, other) * edges, edges)
            return copy(big, full[phase][0].at[pl.ds(at, edges)], big_sem.at[0])

        def node_copy(phase):
            at = pl.multiple_of(jnp.where(sec == rounds[phase], gi, other) * nodes, nodes)
            return copy(nf.at[phase % 2], full[phase][1].at[pl.ds(at, nodes)], node_sems.at[phase])

        def low_copies(phase):
            kind = jnp.where(sec == 0, 0, 1) if phase == 1 else phase // 2
            return (
                copy(lows[phase], send_e.at[kind, which], low_sems.at[phase]),
                copy(nlow.at[phase % 2], send_n.at[kind, which], nlow_sems.at[phase]),
            )

        def low_start(phase, k):
            if phase > 0 and (phase, k) != (2, 0):
                low_copies(phase - 1)[k].wait()
            if phase < 3:
                low_copies(phase)[k].start()
            else:

                @pl.when(sec != rounds[phase])
                def _():
                    low_copies(phase)[k].start()

        def nodes_out(phase, here, out):
            nf[phase % 2, here, :] = out
            nlow[phase % 2, here, :] = out.astype(BF16)

        def drain():
            big_copy(3).wait()
            for phase in (2, 3):
                node_copy(phase).wait()

            @pl.when(sec != rounds[3])
            def _():
                for c in low_copies(3):
                    c.wait()

        loads = [
            copy(edge_hbm.at[pl.ds(erow, edges)], es.at[:, own[0]], load_sems.at[0]),
            copy(node_hbm.at[pl.ds(nrow, nodes)], h0_in, load_sems.at[1]),
            copy(ncot_hbm.at[pl.ds(nrow, nodes)], cotn, load_sems.at[3]),
        ]
        load_cot = copy(ecot_hbm.at[pl.ds(erow, edges)], cot, load_sems.at[2])
        for c in loads:
            c.start()

        rows = edges // 128
        irow = pl.multiple_of(gi * rows, rows)

        one, zero = jnp.ones((128, 128), BF16), jnp.zeros((128, 128), BF16)

        def build(j):
            at = slice(j * 128, (j + 1) * 128)
            for k, idx in enumerate((idx_s, idx_r)):
                row = idx[pl.ds(irow + j, 1), :]
                ahead = jnp.broadcast_to(row, (16, 128)) - lax.broadcasted_iota(jnp.int32, (16, 128), 0)
                ahead = ahead.astype(jnp.int16)
                for c in range(0, nodes, 16):
                    hit = jnp.where(ahead == jnp.int16(c), one[:16], zero[:16])
                    srt[k * nodes + c : k * nodes + c + 16, at] = hit
                column = jnp.broadcast_to(row, (128, 128)).T
                ahead = (column - lax.broadcasted_iota(jnp.int32, (128, 128), 1)).astype(jnp.int16)
                for c in range(0, nodes, 128):
                    to = col_s + k * nodes + c
                    es[at, to : to + 128] = jnp.where(ahead == jnp.int16(c), one, zero)

        @pl.when(which == 0)
        def _():
            copy(w_mine, wv.at[0], load_sems.at[4]).wait()
            copy(w_mine, wv.at[1], load_sems.at[5]).wait()
            for r in range(2):
                we, _, w2, _, w4 = weights(r)
                wc[r, :width, :] = centre(w2)
                wc[r, width : 2 * width, :] = centre(w4)
                wc[r, 2 * width : 3 * width, :] = (w2.astype(F32) * 0.5).T.astype(BF16)
                wc[r, 3 * width :, :] = we.astype(F32).T.astype(BF16)

        @pl.when(which > 0)
        def _():
            drain()

        for c in loads:
            c.wait()

        def forward_table(r, hl):
            we, wsr, _, _, _ = weights(r)
            jn[r, :, :width] = hl
            k_e, k_s = (0, width) if r == 0 else (2 * nodes, 0)
            pw[k_e : k_e + width, :] = we * 0.5
            table = dot(hl, wsr) * 0.5
            pw[k_s : k_s + nodes, :] = table[:, :width].astype(BF16)
            pw[k_s + nodes : k_s + 2 * nodes, :] = (table[:, width:] + vec(r, 0) * 0.5).astype(BF16)

        def forward(r, h):
            phase = r
            forward_table(r, h.astype(BF16))
            _, _, _, w3, _ = weights(r)
            b2 = vec(r, 1)
            b2c = b2 - row_mean(b2)
            gain, shift = vec(r, 2), vec(r, 3)
            lo = lows[phase]
            message = (xh1, cot)[r]
            if phase > 0:
                big_copy(phase - 1).wait()

            def block(i):
                here = slice(i * n, (i + 1) * n)
                if r == 0:
                    for j in range(i * n // 128, (i + 1) * n // 128):
                        build(j)
                    yield
                half = dot(es[here, spans[r]], pw[...])
                yield
                act, slope = half_silu(half)
                act = act.astype(BF16)
                acts[r][:, here] = act.T
                dds[r][here, :] = slope.astype(BF16)
                yield
                z = dot(act, wc[r, :width, :])
                yield
                z = z + b2c
                inv = lax.rsqrt(row_mean(z * z) + EPS)
                xh = z * inv
                xhs[r][here, :] = xh.astype(BF16)
                inv_e[here, lanes[r]] = jnp.broadcast_to(inv, (n, 64)).astype(BF16)
                update = xh * gain + shift
                message[here, :] = update.astype(BF16)
                out = es[here, own[r]].astype(F32) + update
                big[here, :] = out
                lo[here, :] = out.astype(BF16)
                yield
                if (i + 1) * n % CHUNK == 0:
                    part = slice((i + 1) * n - CHUNK, (i + 1) * n)
                    add = dot(srt[nodes:, part], message[part, :])
                    acc[:nodes, :] = add if part.start == 0 else acc[:nodes, :] + add
                    yield

            interleave([block(i) for i in range(edges // n)], 1)
            big_copy(phase).start()
            low_start(phase, 0)
            if r == 1:
                load_cot.start()
            b4 = vec(r, 5)
            b4c = b4 - row_mean(b4)
            b3 = vec(r, 4)

            def node_block(i):
                here = slice(i * half_n, (i + 1) * half_n)
                jn[r, here, width:] = acc[here, :].astype(BF16)
                z = dot(jn[r, here, :], w3)
                yield
                act, slope = half_silu((z + b3) * 0.5)
                act = act.astype(BF16)
                act_n[r, here, :] = act
                slope_n[r, here, :] = slope.astype(BF16)
                z = dot(act, wc[r, width : 2 * width, :])
                yield
                z = z + b4c
                inv = lax.rsqrt(row_mean(z * z) + EPS)
                xh = z * inv
                xh_n[r, here, :] = xh.astype(BF16)
                inv_n[r, here, :] = jnp.broadcast_to(inv, (half_n, 128))
                h_here = h[here, :] if r == 0 else nf[0, here, :]
                nodes_out(phase, here, h_here + xh * vec(r, 6) + vec(r, 7))
                yield

            interleave([node_block(i) for i in range(2)], 1)
            node_copy(phase).start()
            low_start(phase, 1)
            return nf[phase % 2]

        def backward(r, de_ref, dn, before):
            phase = 3 - r
            _, wsr, _, w3, w4 = weights(r)
            gain_n = vec(r, 6)
            d4s, d3s, djs = {}, {}, {}

            def node_block(i):
                here = slice(i * half_n, (i + 1) * half_n)
                xh = xh_n[r, here, :].astype(F32)
                g = dn[here, :] * gain_n
                d4 = inv_n[r, here, :1] * (g - row_mean(g) - xh * row_mean(g * xh))
                d4s[i] = d4.astype(BF16)
                d3 = dot_nt(d4s[i], w4)
                yield
                d3s[i] = (d3 * slope_n[r, here, :].astype(F32) * 0.5).astype(BF16)
                djs[i] = dot_nt(d3s[i], w3)
                yield

            def extra():
                for job in before:
                    job()
                    yield

            interleave([node_block(0), node_block(1), extra()], 1)
            djn = jnp.concatenate([djs[0], djs[1]], axis=0)
            dtotal = djn[:, width:].astype(BF16)
            dh_own[...] = djn[:, :width]
            d4 = jnp.concatenate([d4s[0], d4s[1]], axis=0)
            d3 = jnp.concatenate([d3s[0], d3s[1]], axis=0)
            put_w(r, 6 * width, dot_tn(act_n[r], d4))
            put_w(r, 4 * width, dot_tn(jn[r], d3))
            put_v(r, 6, col_sum(dn * xh_n[r].astype(F32)))
            put_v(r, 7, col_sum(dn))
            put_v(r, 5, col_sum(d4.astype(F32)))
            put_v(r, 4, col_sum(d3.astype(F32)))
            gain = vec(r, 2)
            w2t = wc[r, 2 * width : 3 * width, :]
            wet = wc[r, 3 * width :, :]
            lo = lows[phase]
            sums = [jnp.zeros((1, width), F32)] * 3
            big_copy(phase - 1).wait()

            def block(i):
                here = slice(i * n, (i + 1) * n)
                g = dot(es[here, col_r:col_1], dtotal)
                yield
                xh = xhs[r][here, :].astype(F32)
                inv = inv_e[here, lanes[r]][:, :1].astype(F32)
                g = (de_ref[here, :].astype(F32) + g) * gain
                gx = g * xh
                d2 = inv * (g - row_mean(g) - xh * row_mean(gx))
                for k, value in enumerate((gx, g, d2)):
                    sums[k] = sums[k] + col_sum(value)
                d2 = d2.astype(BF16)
                xhs[r][here, :] = d2
                yield
                d1 = dot(d2, w2t)
                yield
                d1 = (d1 * dds[r][here, :].astype(F32)).astype(BF16)
                dds[r][here, :] = d1
                yield
                back = dot(d1, wet)
                yield
                out = de_ref[here, :].astype(F32) + back
                big[here, :] = out
                lo[here, :] = out.astype(BF16)
                yield
                if (i + 1) * n % CHUNK == 0:
                    part = slice((i + 1) * n - CHUNK, (i + 1) * n)
                    add = dot(srt[:, part], dds[r][part, :])
                    acc[...] = add if part.start == 0 else acc[...] + add
                    yield
                    put_w(r, 3 * width, dot(acts[r][:, part], xhs[r][part, :]))
                    put_w(r, 0, dot_tn(es[part, own[r]], dds[r][part, :]))
                    yield

            interleave([block(i) for i in range(edges // n)], 1)
            big_copy(phase).start()
            low_start(phase, 0)
            both = jnp.concatenate([acc[:nodes, :], acc[nodes:, :]], axis=1).astype(BF16)
            node_copy(phase - 2).wait()
            nodes_out(phase, slice(0, nodes), dn + dh_own[...] + dot_nt(both, wsr))
            node_copy(phase).start()
            low_start(phase, 1)

            def sums_out():
                put_v(r, 2, sums[0] / gain)
                put_v(r, 3, sums[1] / gain)
                put_v(r, 1, sums[2])
                put_v(r, 0, col_sum(both[:, width:].astype(F32)))

            def table_out():
                dws = dot_tn(jn[r, :, :width], both)
                put_w(r, width, dws[:, :width])
                put_w(r, 2 * width, dws[:, width:])

            return nf[phase % 2], (sums_out, table_out)

        h1 = forward(0, h0_in[...].astype(F32))
        forward(1, h1)
        load_cot.wait()
        low_copies(1)[0].wait()
        dn, jobs = backward(1, cot, cotn[...].astype(F32), ())
        _, jobs = backward(0, low, dn, jobs)
        for job in jobs:
            job()

        @pl.when(which == GRAPHS - 1)
        def _():
            drain()

        return carry

    lax.fori_loop(0, GRAPHS, graph, 0)
    wl = dd0.at[:GRAD_ROWS]

    for r in range(2):

        @pl.when(sec == r)
        def _(r=r):
            copy(wg.at[r], wg_keep, grad_sems.at[0]).start()

        @pl.when(sec != r)
        def _(r=r):
            wl[...] = wg[r].astype(BF16)
            copy(wl, wg_send, grad_sems.at[1]).start()

    copy(wg.at[0], wg_keep, grad_sems.at[0]).wait()
    copy(wl, wg_send, grad_sems.at[1]).wait()


def run_graphs(nodes, edges, sec, idx_s, idx_r, node, edge, ncot, ecot, w_mine, w_theirs, v_mine, v_theirs):
    width = node.shape[1]
    any_spec = pl.BlockSpec(memory_space=pl.ANY)
    vmem = pl.BlockSpec(memory_space=pltpu.VMEM)
    smem = pl.BlockSpec(memory_space=pltpu.SMEM)
    shape = jax.ShapeDtypeStruct
    whole = [shape((edge.shape[0], width), F32), shape((node.shape[0], width), F32)]
    outs = (
        *whole,
        *whole,
        shape((2, GRAPHS, edges, width), BF16),
        shape((2, GRAPHS, nodes, width), BF16),
        shape((GRAD_ROWS, width), F32),
        shape((GRAD_ROWS, width), BF16),
    )
    return pl.pallas_call(
        functools.partial(graphs_kernel, nodes, edges, width),
        out_shape=outs,
        in_specs=[smem, vmem, vmem] + [any_spec] * 6 + [vmem, vmem],
        out_specs=(any_spec,) * 8,
        scratch_shapes=[
            pltpu.VMEM((edges, 2 * width + 2 * nodes), BF16),
            pltpu.VMEM((2 * nodes, edges), BF16),
            *[pltpu.VMEM((edges, width), BF16)] * 2,
            *[pltpu.VMEM((width, edges), BF16)] * 2,
            *[pltpu.VMEM((edges, width), BF16)] * 4,
            pltpu.VMEM((edges, 128), BF16),
            pltpu.VMEM((edges, width), F32),
            pltpu.VMEM((2, w_mine.shape[0], width), BF16),
            pltpu.VMEM((2, 4 * width, width), BF16),
            pltpu.VMEM((2, 8, width), F32),
            pltpu.VMEM((nodes, width), BF16),
            pltpu.VMEM((nodes, width), BF16),
            pltpu.VMEM((2, nodes, width), F32),
            pltpu.VMEM((2, nodes, width), BF16),
            pltpu.VMEM((2 * nodes, width), F32),
            pltpu.VMEM((nodes, width), F32),
            pltpu.VMEM((2 * nodes + width, width), BF16),
            pltpu.VMEM((2, nodes, 2 * width), BF16),
            *[pltpu.VMEM((2, nodes, width), BF16)] * 3,
            pltpu.VMEM((2, nodes, 128), F32),
            pltpu.VMEM((2, GRAD_ROWS, width), F32),
            pltpu.SemaphoreType.DMA((8,)),
            pltpu.SemaphoreType.DMA((1,)),
            *[pltpu.SemaphoreType.DMA((4,))] * 3,
            pltpu.SemaphoreType.DMA((2,)),
        ],
        compiler_params=pltpu.CompilerParams(vmem_limit_bytes=60 * 2**20),
        cost_estimate=pl.CostEstimate(flops=80 * 2 * edges * width * width, transcendentals=0, bytes_accessed=2**25),
        name="graphs",
    )(sec, idx_s, idx_r, node, edge, ncot, ecot, w_mine, w_theirs, v_mine, v_theirs)


def spread_kernel(kind, nodes, edges, rows, sec_ref, recv_e, recv_n, *rest):
    out_e, out_n, e_in, n_in, e_out, n_out, in_sems, out_sems = rest[2:]
    start = GRAPHS * (1 - sec_ref[0])
    parts = []
    for g in range(GRAPHS):
        at = pl.multiple_of((start + g) * nodes, nodes)
        parts.append((recv_n.at[kind, g], n_in.at[g], n_out.at[g], out_n.at[pl.ds(at, nodes)]))
        for i in range(edges // rows):
            here = pl.ds(i * rows, rows)
            at = pl.multiple_of((start + g) * edges + i * rows, rows)
            parts.append((recv_e.at[kind, g, here], e_in.at[g, here], e_out.at[g, here], out_e.at[pl.ds(at, rows)]))
    reads = [pltpu.make_async_copy(p[0], p[1], in_sems.at[i]) for i, p in enumerate(parts)]
    writes = [pltpu.make_async_copy(p[2], p[3], out_sems.at[i]) for i, p in enumerate(parts)]
    for c in reads:
        c.start()
    for p, r, w in zip(parts, reads, writes):
        r.wait()
        p[2][...] = p[1][...].astype(F32)
        w.start()
    for w in writes:
        w.wait()


def spread(kind, nodes, edges, sec, recv_e, recv_n, full):
    width = recv_e.shape[-1]
    rows = 1024
    count = GRAPHS * (edges // rows + 1)
    any_spec = pl.BlockSpec(memory_space=pl.ANY)
    return pl.pallas_call(
        functools.partial(spread_kernel, kind, nodes, edges, rows),
        out_shape=tuple(jax.ShapeDtypeStruct(f.shape, f.dtype) for f in full),
        in_specs=[pl.BlockSpec(memory_space=pltpu.SMEM)] + [any_spec] * 4,
        out_specs=(any_spec,) * 2,
        input_output_aliases={3 + i: i for i in range(2)},
        scratch_shapes=[
            pltpu.VMEM((GRAPHS, edges, width), BF16),
            pltpu.VMEM((GRAPHS, nodes, width), BF16),
            pltpu.VMEM((GRAPHS, edges, width), F32),
            pltpu.VMEM((GRAPHS, nodes, width), F32),
            pltpu.SemaphoreType.DMA((count,)),
            pltpu.SemaphoreType.DMA((count,)),
        ],
        compiler_params=pltpu.CompilerParams(vmem_limit_bytes=24 * 2**20),
        cost_estimate=pl.CostEstimate(flops=0, transcendentals=0, bytes_accessed=12 * (edges + nodes) * width),
        name="spread",
    )(sec, recv_e, recv_n, *full)


def reduce_over_dp(value, beside):
    devices = lax.axis_size("dp")
    sec = lax.axis_index("section")
    me = lax.axis_index("dp")
    bits = [1 << k for k in range(devices.bit_length() - 1)]
    orders = [bits, bits[:2][::-1] + bits[2:]]
    halved = min(2, len(bits))
    count = [0]

    def swap(part, step):
        pairs = [
            (s * devices + i, s * devices + (i ^ orders[s][step]))
            for s in range(2)
            for i in range(devices)
        ]
        part = part.astype(BF16)
        got = lax.ppermute(part, ("section", "dp"), pairs)
        if count[0] in beside:
            got = beside[count[0]](part, got)
        count[0] += 1
        return got.astype(F32)

    def high(step):
        return jnp.where(sec == 0, me // orders[0][step], me // orders[1][step]) % 2

    part = value
    for step in range(halved):
        half = part.shape[0] // 2
        mine = high(step)
        keep = lax.dynamic_slice_in_dim(part, mine * half, half, 0)
        send = lax.dynamic_slice_in_dim(part, (1 - mine) * half, half, 0)
        part = keep + swap(send, step)
    for step in range(halved, len(bits)):
        part = part + swap(part, step)
    for step in reversed(range(halved)):
        got = swap(part, step)
        if step == 0:
            return part, got, high(0)
        part = jnp.where(
            high(step) == 0, jnp.concatenate([part, got], 0), jnp.concatenate([got, part], 0)
        )
    return part[: value.shape[0] // 2], part[value.shape[0] // 2 :], jnp.zeros((), jnp.int32)


def place_kernel(flag_ref, part_ref, got_ref, *outs):
    own = flag_ref[0] == 0
    rows = part_ref.shape[0]
    at = 0
    for out in outs:
        end = at + out.shape[0]
        if at < rows:
            stop = min(end, rows)
            out[: stop - at, :] = jnp.where(own, part_ref[at:stop, :], got_ref[at:stop, :])
        if end > rows:
            start = max(at, rows)
            here = slice(start - rows, end - rows)
            out[start - at :, :] = jnp.where(own, got_ref[here, :], part_ref[here, :])
        at = end


def place(part, got, flag, sizes):
    vmem = pl.BlockSpec(memory_space=pltpu.VMEM)
    return pl.pallas_call(
        place_kernel,
        out_shape=tuple(jax.ShapeDtypeStruct((rows, part.shape[1]), F32) for rows in sizes),
        in_specs=[pl.BlockSpec(memory_space=pltpu.SMEM), vmem, vmem],
        out_specs=(vmem,) * len(sizes),
        compiler_params=pltpu.CompilerParams(vmem_limit_bytes=16 * 2**20),
        name="place",
    )(flag.reshape(1).astype(jnp.int32), part, got)


def shards(
    node_input,
    edge_input,
    senders,
    receivers,
    node_cot,
    edge_cot,
    edge_w1,
    edge_b1,
    edge_w2,
    edge_b2,
    edge_gain,
    edge_shift,
    node_w1,
    node_b1,
    node_w2,
    node_b2,
    node_gain,
    node_shift,
):
    nodes = node_input.shape[0] // MICRO
    edges = edge_input.shape[0] // MICRO
    width = node_input.shape[1]
    sec = lax.axis_index("section").reshape(1).astype(jnp.int32)
    other = [(0, 1), (1, 0)]
    w_mine = jnp.concatenate([edge_w1[0], edge_w2[0], node_w1[0], node_w2[0]], axis=0)
    v_mine = jnp.concatenate(
        [edge_b1, edge_b2, edge_gain, edge_shift, node_b1, node_b2, node_gain, node_shift], axis=0
    )
    w_theirs = lax.ppermute(w_mine, "section", other)
    v_theirs = lax.ppermute(v_mine, "section", other)
    idx_s = senders.reshape(-1, 128)
    idx_r = receivers.reshape(-1, 128)
    out = run_graphs(
        nodes,
        edges,
        sec,
        idx_s,
        idx_r,
        node_input,
        edge_input,
        node_cot,
        edge_cot,
        w_mine,
        w_theirs,
        v_mine,
        v_theirs,
    )
    full = [out[:2], out[2:4]]
    mine = out[6] + lax.ppermute(out[7], "section", other).astype(F32)
    sent, mine = lax.optimization_barrier((out[4:6], mine))
    recv = tuple(lax.ppermute(x, "section", other) for x in sent)

    def fill(kind):
        def run(sent, came):
            sent, here, whole = lax.optimization_barrier((sent, recv, full[kind]))
            full[kind] = spread(kind, nodes, edges, sec, *here, whole)
            came, full[kind] = lax.optimization_barrier((came, full[kind]))
            return came

        return run

    total = reduce_over_dp(mine, {3: fill(0), 5: fill(1)})
    (lat_e, lat_n), (gr_e, gr_n) = full
    out = place(*total, (3 * width, width, 2 * width, width) + (1,) * 8)
    w1, w2, n1, n2 = (w[None] for w in out[:4])
    return (
        lat_n[None],
        lat_e[None],
        gr_n[None],
        gr_e[None],
        w1,
        out[4],
        w2,
        out[5],
        out[6],
        out[7],
        n1,
        out[8],
        n2,
        out[9],
        out[10],
        out[11],
    )


def solution(mesh):
    rows = P("dp", None)
    mat = P("section", None, None)
    row = P("section", None)
    in_specs = (rows, rows, P("dp"), P("dp"), rows, rows) + (mat, row, mat, row, row, row) * 2
    whole = P("section", "dp", None)
    out_specs = (whole,) * 4 + (mat, row, mat, row, row, row) * 2
    return jax.shard_map(shards, mesh=mesh, in_specs=in_specs, out_specs=out_specs, check_vma=False)
```

```python
import functools

import jax
import jax.numpy as jnp
from jax import lax
from jax.experimental import pallas as pl
from jax.experimental.pallas import tpu as pltpu
from jax.sharding import PartitionSpec as P

MICRO = 4
GRAPHS = 2
EPS = 1e-05
BLOCK = 256
NODE_BLOCKS = 1
CHUNK = 1024
GRAD_ROWS = 1856
F32 = jnp.float32
BF16 = jnp.bfloat16


def dot(left, right):
    return jnp.dot(left, right, preferred_element_type=F32)


def dot_tn(left, right):
    return lax.dot_general(left, right, (((0,), (0,)), ((), ())), preferred_element_type=F32)


def dot_nt(left, right):
    return lax.dot_general(left, right, (((1,), (1,)), ((), ())), preferred_element_type=F32)


def col_sum(value):
    return jnp.sum(value, axis=0, keepdims=True)


def row_mean(value):
    return jnp.mean(value, axis=1, keepdims=True)


def half_silu(half):
    t = jnp.tanh(half)
    up = 1.0 + t
    act = half * up
    return act, up + act * (1.0 - t)


def twice(lanes):
    return jnp.concatenate([lanes, lanes], axis=1)


def eight_rows(value):
    return jnp.sum(value.reshape(-1, 8, value.shape[1]), axis=0)


def centre(w):
    w = w.astype(F32)
    return (w - row_mean(w)).astype(BF16)


def interleave(parts, skew):
    parts = list(parts)
    done = [False] * len(parts)
    clock = 0
    while not all(done):
        for i, part in enumerate(parts):
            if clock >= i * skew and not done[i]:
                done[i] = next(part, "end") == "end"
        clock += 1


def graphs_kernel(
    nodes,
    edges,
    width,
    sec_ref,
    idx_s,
    idx_r,
    node_hbm,
    edge_hbm,
    ncot_hbm,
    ecot_hbm,
    w_mine,
    w_theirs,
    v_mine,
    v_theirs,
    lat_e,
    lat_n,
    gr_e,
    gr_n,
    send_e,
    send_n,
    wg_keep,
    wg_send,
    es,
    srt,
    cot,
    low,
    act0,
    act1,
    dd0,
    dd1,
    xh0,
    xh1,
    inv0,
    inv1,
    big,
    wv,
    wc,
    vs,
    h0_in,
    cotn,
    nf,
    nlow,
    acc,
    dh_own,
    pw,
    jn,
    act_n,
    slope_n,
    xh_n,
    inv_n,
    wg,
    load_sems,
    big_sems,
    node_sems,
    low_sems,
    nlow_sems,
    grad_sems,
):
    acts, dds, xhs, invs = (act0, act1), (dd0, dd1), (xh0, xh1), (inv0, inv1)
    sec = sec_ref[0]
    first = sec == 0
    n = BLOCK
    rows_n = nodes // NODE_BLOCKS
    node_rows = [slice(i * rows_n, (i + 1) * rows_n) for i in range(NODE_BLOCKS)]
    col_s, col_r, col_1 = width, width + nodes, width + 2 * nodes
    spans = (slice(0, col_1), slice(col_s, col_1 + width))
    own = (slice(0, width), slice(col_1, col_1 + width))
    copy = pltpu.make_async_copy
    rounds = (0, 1, 1, 0)
    full = ((lat_e, lat_n), (lat_e, lat_n), (gr_e, gr_n), (gr_e, gr_n))
    lows = (es.at[:, own[1]], low, low, cot)

    @pl.when(first)
    def _():
        copy(w_mine, wv.at[0], load_sems.at[4]).start()
        copy(w_theirs, wv.at[1], load_sems.at[5]).start()

    @pl.when(jnp.logical_not(first))
    def _():
        copy(w_theirs, wv.at[0], load_sems.at[4]).start()
        copy(w_mine, wv.at[1], load_sems.at[5]).start()

    vs[0] = jnp.where(first, v_mine[...], v_theirs[...])
    vs[1] = jnp.where(first, v_theirs[...], v_mine[...])
    wg[...] = jnp.zeros_like(wg)

    def vec(r, k):
        return vs[r, k : k + 1, :]

    def weights(r):
        w1 = [wv[r, k * width : (k + 1) * width, :] for k in range(3)]
        at = 3 * width
        return (
            w1[0],
            jnp.concatenate(w1[1:], axis=1),
            wv[r, at : at + width, :],
            wv[r, at + width : at + 3 * width, :],
            wv[r, at + 3 * width : at + 4 * width, :],
        )

    def put_w(r, at, value):
        here = slice(at, at + value.shape[0])
        wg[r, here, :] = wg[r, here, :] + value

    def put_v(r, k, value):
        put_w(r, 7 * width + k, value)

    def graph(which, carry):
        gi = 2 * sec + which
        other = 2 * (1 - sec) + which
        erow = pl.multiple_of(gi * edges, edges)
        nrow = pl.multiple_of(gi * nodes, nodes)

        def big_copy(phase, k):
            at = pl.multiple_of(jnp.where(sec == rounds[phase], gi, other) * edges, edges) + k * CHUNK
            here = pl.ds(pl.multiple_of(at, CHUNK), CHUNK)
            return copy(big.at[pl.ds(k * CHUNK, CHUNK)], full[phase][0].at[here], big_sems.at[k])

        def big_wait(phase):
            for k in range(edges // CHUNK):
                big_copy(phase, k).wait()

        def node_copy(phase):
            at = pl.multiple_of(jnp.where(sec == rounds[phase], gi, other) * nodes, nodes)
            return copy(nf.at[phase % 2], full[phase][1].at[pl.ds(at, nodes)], node_sems.at[phase])

        def low_copies(phase):
            kind = jnp.where(sec == 0, 0, 1) if phase == 1 else phase // 2
            return (
                copy(lows[phase], send_e.at[kind, which], low_sems.at[phase]),
                copy(nlow.at[phase % 2], send_n.at[kind, which], nlow_sems.at[phase]),
            )

        def low_start(phase, k):
            if phase > 0 and (phase, k) != (2, 0):
                low_copies(phase - 1)[k].wait()
            if phase < 3:
                low_copies(phase)[k].start()
            else:

                @pl.when(sec != rounds[phase])
                def _():
                    low_copies(phase)[k].start()

        def nodes_out(phase, here, out):
            nf[phase % 2, here, :] = out
            nlow[phase % 2, here, :] = out.astype(BF16)

        def drain():
            big_wait(3)
            for phase in (2, 3):
                node_copy(phase).wait()

            @pl.when(sec != rounds[3])
            def _():
                for c in low_copies(3):
                    c.wait()

        loads = [
            copy(edge_hbm.at[pl.ds(erow, edges)], es.at[:, own[0]], load_sems.at[0]),
            copy(node_hbm.at[pl.ds(nrow, nodes)], h0_in, load_sems.at[1]),
            copy(ncot_hbm.at[pl.ds(nrow, nodes)], cotn, load_sems.at[3]),
        ]
        load_cot = copy(ecot_hbm.at[pl.ds(erow, edges)], cot, load_sems.at[2])
        for c in loads:
            c.start()

        rows = edges // 128
        irow = pl.multiple_of(gi * rows, rows)

        one, zero = jnp.ones((128, 128), BF16), jnp.zeros((128, 128), BF16)

        def build(j):
            at = slice(j * 128, (j + 1) * 128)
            for k, idx in enumerate((idx_s, idx_r)):
                row = idx[pl.ds(irow + j, 1), :]
                ahead = jnp.broadcast_to(row, (16, 128)) - lax.broadcasted_iota(jnp.int32, (16, 128), 0)
                ahead = ahead.astype(jnp.int16)
                for c in range(0, nodes, 16):
                    hit = jnp.where(ahead == jnp.int16(c), one[:16], zero[:16])
                    srt[k * nodes + c : k * nodes + c + 16, at] = hit
                column = jnp.broadcast_to(row, (128, 128)).T
                ahead = (column - lax.broadcasted_iota(jnp.int32, (128, 128), 1)).astype(jnp.int16)
                for c in range(0, nodes, 128):
                    to = col_s + k * nodes + c
                    es[at, to : to + 128] = jnp.where(ahead == jnp.int16(c), one, zero)

        @pl.when(which == 0)
        def _():
            copy(w_mine, wv.at[0], load_sems.at[4]).wait()
            copy(w_mine, wv.at[1], load_sems.at[5]).wait()
            for r in range(2):
                we, _, w2, _, w4 = weights(r)
                wc[r, :width, :] = centre(w2)
                wc[r, width : 2 * width, :] = centre(w4)
                wc[r, 2 * width : 3 * width, :] = (w2.astype(F32) * 0.5).T.astype(BF16)
                wc[r, 3 * width :, :] = we.astype(F32).T.astype(BF16)

        @pl.when(which > 0)
        def _():
            drain()

        for c in loads:
            c.wait()

        def forward_table(r, here, h):
            _, wsr, _, _, _ = weights(r)
            hl = h.astype(BF16)
            jn[r, here, :width] = hl
            k_s = width if r == 0 else 0
            table = dot(hl, wsr) * 0.5
            pw[k_s + here.start : k_s + here.stop, :] = table[:, :width].astype(BF16)
            to = k_s + nodes
            pw[to + here.start : to + here.stop, :] = (table[:, width:] + vec(r, 0) * 0.5).astype(BF16)

        def forward(r, h):
            phase = r
            we, _, _, w3, _ = weights(r)
            k_e = 0 if r == 0 else 2 * nodes
            pw[k_e : k_e + width, :] = we * 0.5
            if r == 0:
                for here in node_rows:
                    forward_table(0, here, h(here))
            b2 = vec(r, 1)
            b2c = b2 - row_mean(b2)
            gain, shift = vec(r, 2), vec(r, 3)
            lo = lows[phase]
            message = (xh1, cot)[r]
            if phase > 0:
                big_wait(phase - 1)

            def block(i):
                here = slice(i * n, (i + 1) * n)
                if r == 0:
                    for j in range(i * n // 128, (i + 1) * n // 128):
                        build(j)
                    yield
                half = dot(es[here, spans[r]], pw[...])
                yield
                act, slope = half_silu(half)
                act = act.astype(BF16)
                acts[r][:, here] = act.T
                dds[r][here, :] = slope.astype(BF16)
                yield
                z = dot(act, wc[r, :width, :])
                yield
                z = z + b2c
                inv = lax.rsqrt(row_mean(z * z) + EPS)
                xh = z * inv
                xhs[r][here, :] = xh.astype(BF16)
                invs[r][here, :] = jnp.broadcast_to(inv, (n, 128)).astype(BF16)
                update = xh * gain + shift
                message[here, :] = update.astype(BF16)
                out = es[here, own[r]].astype(F32) + update
                big[here, :] = out
                lo[here, :] = out.astype(BF16)
                yield
                if (i + 1) * n % CHUNK == 0:
                    part = slice((i + 1) * n - CHUNK, (i + 1) * n)
                    big_copy(phase, i * n // CHUNK).start()
                    add = dot(srt[nodes:, part], message[part, :])
                    acc[:nodes, :] = add if part.start == 0 else acc[:nodes, :] + add
                    yield

            interleave([block(i) for i in range(edges // n)], 1)
            low_start(phase, 0)
            if r == 1:
                load_cot.start()
            b4 = vec(r, 5)
            b4c = b4 - row_mean(b4)
            b3 = vec(r, 4)

            def node_block(here):
                jn[r, here, width:] = acc[here, :].astype(BF16)
                z = dot(jn[r, here, :], w3)
                yield
                act, slope = half_silu((z + b3) * 0.5)
                act = act.astype(BF16)
                act_n[r, here, :] = act
                slope_n[r, here, :] = slope.astype(BF16)
                z = dot(act, wc[r, width : 2 * width, :])
                yield
                z = z + b4c
                inv = lax.rsqrt(row_mean(z * z) + EPS)
                xh = z * inv
                xh_n[r, here, :] = xh.astype(BF16)
                inv_n[r, here, :] = jnp.broadcast_to(inv, (rows_n, 128))
                out = h(here) + xh * vec(r, 6) + vec(r, 7)
                nodes_out(phase, here, out)
                if r == 0:
                    forward_table(1, here, out)
                yield

            interleave([node_block(here) for here in node_rows], 1)
            node_copy(phase).start()
            low_start(phase, 1)

        def backward(r, de_ref, dn_rows, before):
            phase = 3 - r
            _, wsr, _, w3, w4 = weights(r)
            gain_n = vec(r, 6)
            dns, d4s, d3s, djs = [], [], [], []

            def node_block(here):
                dn = dn_rows(here)
                dns.append(dn)
                yield
                xh = xh_n[r, here, :].astype(F32)
                g = dn * gain_n
                d4 = twice(inv_n[r, here, :]) * (g - row_mean(g) - xh * row_mean(g * xh))
                d4s.append(d4.astype(BF16))
                d3 = dot_nt(d4s[-1], w4)
                yield
                d3s.append((d3 * slope_n[r, here, :].astype(F32) * 0.5).astype(BF16))
                djn = dot_nt(d3s[-1], w3)
                yield
                djs.append(djn[:, width:].astype(BF16))
                dh_own[here, :] = djn[:, :width]
                yield

            interleave([node_block(here) for here in node_rows], 1)
            if phase == 3:
                node_copy(2).start()
                low_start(2, 1)
            for job in before:
                job()
            dtotal, d4, d3, dn = (jnp.concatenate(x, axis=0) for x in (djs, d4s, d3s, dns))
            put_w(r, 6 * width, dot_tn(act_n[r], d4))
            put_w(r, 4 * width, dot_tn(jn[r], d3))
            put_v(r, 6, col_sum(dn * xh_n[r].astype(F32)))
            put_v(r, 7, col_sum(dn))
            put_v(r, 5, col_sum(d4.astype(F32)))
            put_v(r, 4, col_sum(d3.astype(F32)))
            gain = vec(r, 2)
            w2t = wc[r, 2 * width : 3 * width, :]
            wet = wc[r, 3 * width :, :]
            lo = lows[phase]
            sums = [jnp.zeros((8, width), F32)] * 3
            big_wait(phase - 1)

            def block(i):
                here = slice(i * n, (i + 1) * n)
                g = dot(es[here, col_r:col_1], dtotal)
                yield
                xh = xhs[r][here, :].astype(F32)
                inv = twice(invs[r][here, :].astype(F32))
                g = (de_ref[here, :].astype(F32) + g) * gain
                gx = g * xh
                d2 = inv * (g - row_mean(g) - xh * row_mean(gx))
                for k, value in enumerate((gx, g, d2)):
                    sums[k] = sums[k] + eight_rows(value)
                d2 = d2.astype(BF16)
                xhs[r][here, :] = d2
                yield
                d1 = dot(d2, w2t)
                yield
                d1 = (d1 * dds[r][here, :].astype(F32)).astype(BF16)
                dds[r][here, :] = d1
                yield
                back = dot(d1, wet)
                yield
                out = de_ref[here, :].astype(F32) + back
                big[here, :] = out
                lo[here, :] = out.astype(BF16)
                yield
                if (i + 1) * n % CHUNK == 0:
                    part = slice((i + 1) * n - CHUNK, (i + 1) * n)
                    big_copy(phase, i * n // CHUNK).start()
                    put_w(r, 3 * width, dot(acts[r][:, part], xhs[r][part, :]))
                    yield
                    for half in (slice(0, nodes), slice(nodes, 2 * nodes)):
                        add = dot(srt[half, part], dds[r][part, :])
                        acc[half, :] = add if part.start == 0 else acc[half, :] + add
                        yield
                    put_w(r, 0, dot_tn(es[part, own[r]], dds[r][part, :]))
                    yield

            interleave([block(i) for i in range(edges // n)], 1)
            low_start(phase, 0)
            both = jnp.concatenate([acc[:nodes, :], acc[nodes:, :]], axis=1).astype(BF16)
            node_copy(phase - 2).wait()

            def dn_out(here):
                out = dn_rows(here, True) + dh_own[here, :] + dot_nt(both[here, :], wsr)
                nodes_out(phase, here, out)
                return out

            def sums_out():
                put_v(r, 2, col_sum(sums[0]) / gain)
                put_v(r, 3, col_sum(sums[1]) / gain)
                put_v(r, 1, col_sum(sums[2]))
                put_v(r, 0, col_sum(both[:, width:].astype(F32)))

            def table_out():
                dws = dot_tn(jn[r, :, :width], both)
                put_w(r, width, dws[:, :width])
                put_w(r, 2 * width, dws[:, width:])

            return dn_out, (sums_out, table_out)

        forward(0, lambda here: h0_in[here, :].astype(F32))
        forward(1, lambda here: nf[0, here, :])
        load_cot.wait()
        low_copies(1)[0].wait()
        dn_out, jobs = backward(1, cot, lambda here, again=False: cotn[here, :].astype(F32), ())
        last = lambda here, again=False: nf[0, here, :] if again else dn_out(here)
        dn_out, jobs = backward(0, low, last, jobs)
        for here in node_rows:
            dn_out(here)
        node_copy(3).start()
        low_start(3, 1)
        for job in jobs:
            job()

        @pl.when(which == GRAPHS - 1)
        def _():
            drain()

        return carry

    lax.fori_loop(0, GRAPHS, graph, 0)
    wl = dd0.at[:GRAD_ROWS]

    for r in range(2):

        @pl.when(sec == r)
        def _(r=r):
            copy(wg.at[r], wg_keep, grad_sems.at[0]).start()

        @pl.when(sec != r)
        def _(r=r):
            wl[...] = wg[r].astype(BF16)
            copy(wl, wg_send, grad_sems.at[1]).start()

    copy(wg.at[0], wg_keep, grad_sems.at[0]).wait()
    copy(wl, wg_send, grad_sems.at[1]).wait()


def run_graphs(nodes, edges, sec, idx_s, idx_r, node, edge, ncot, ecot, w_mine, w_theirs, v_mine, v_theirs):
    width = node.shape[1]
    any_spec = pl.BlockSpec(memory_space=pl.ANY)
    vmem = pl.BlockSpec(memory_space=pltpu.VMEM)
    smem = pl.BlockSpec(memory_space=pltpu.SMEM)
    shape = jax.ShapeDtypeStruct
    whole = [shape((edge.shape[0], width), F32), shape((node.shape[0], width), F32)]
    outs = (
        *whole,
        *whole,
        shape((2, GRAPHS, edges, width), BF16),
        shape((2, GRAPHS, nodes, width), BF16),
        shape((GRAD_ROWS, width), F32),
        shape((GRAD_ROWS, width), BF16),
    )
    return pl.pallas_call(
        functools.partial(graphs_kernel, nodes, edges, width),
        out_shape=outs,
        in_specs=[smem, vmem, vmem] + [any_spec] * 6 + [vmem, vmem],
        out_specs=(any_spec,) * 8,
        scratch_shapes=[
            pltpu.VMEM((edges, 2 * width + 2 * nodes), BF16),
            pltpu.VMEM((2 * nodes, edges), BF16),
            *[pltpu.VMEM((edges, width), BF16)] * 2,
            *[pltpu.VMEM((width, edges), BF16)] * 2,
            *[pltpu.VMEM((edges, width), BF16)] * 4,
            *[pltpu.VMEM((edges, 128), BF16)] * 2,
            pltpu.VMEM((edges, width), F32),
            pltpu.VMEM((2, w_mine.shape[0], width), BF16),
            pltpu.VMEM((2, 4 * width, width), BF16),
            pltpu.VMEM((2, 8, width), F32),
            pltpu.VMEM((nodes, width), BF16),
            pltpu.VMEM((nodes, width), BF16),
            pltpu.VMEM((2, nodes, width), F32),
            pltpu.VMEM((2, nodes, width), BF16),
            pltpu.VMEM((2 * nodes, width), F32),
            pltpu.VMEM((nodes, width), F32),
            pltpu.VMEM((2 * nodes + width, width), BF16),
            pltpu.VMEM((2, nodes, 2 * width), BF16),
            *[pltpu.VMEM((2, nodes, width), BF16)] * 3,
            pltpu.VMEM((2, nodes, 128), F32),
            pltpu.VMEM((2, GRAD_ROWS, width), F32),
            pltpu.SemaphoreType.DMA((8,)),
            pltpu.SemaphoreType.DMA((edges // CHUNK,)),
            *[pltpu.SemaphoreType.DMA((4,))] * 3,
            pltpu.SemaphoreType.DMA((2,)),
        ],
        compiler_params=pltpu.CompilerParams(vmem_limit_bytes=60 * 2**20),
        cost_estimate=pl.CostEstimate(flops=80 * 2 * edges * width * width, transcendentals=0, bytes_accessed=2**25),
        name="graphs",
    )(sec, idx_s, idx_r, node, edge, ncot, ecot, w_mine, w_theirs, v_mine, v_theirs)


def spread_kernel(kind, nodes, edges, rows, sec_ref, recv_e, recv_n, *rest):
    out_e, out_n, e_in, n_in, e_out, n_out, in_sems, out_sems = rest[2:]
    start = GRAPHS * (1 - sec_ref[0])
    parts = []
    for g in range(GRAPHS):
        at = pl.multiple_of((start + g) * nodes, nodes)
        parts.append((recv_n.at[kind, g], n_in.at[g], n_out.at[g], out_n.at[pl.ds(at, nodes)]))
        for i in range(edges // rows):
            here = pl.ds(i * rows, rows)
            at = pl.multiple_of((start + g) * edges + i * rows, rows)
            parts.append((recv_e.at[kind, g, here], e_in.at[g, here], e_out.at[g, here], out_e.at[pl.ds(at, rows)]))
    reads = [pltpu.make_async_copy(p[0], p[1], in_sems.at[i]) for i, p in enumerate(parts)]
    writes = [pltpu.make_async_copy(p[2], p[3], out_sems.at[i]) for i, p in enumerate(parts)]
    for c in reads:
        c.start()
    for p, r, w in zip(parts, reads, writes):
        r.wait()
        p[2][...] = p[1][...].astype(F32)
        w.start()
    for w in writes:
        w.wait()


def spread(kind, nodes, edges, sec, recv_e, recv_n, full):
    width = recv_e.shape[-1]
    rows = 1024
    count = GRAPHS * (edges // rows + 1)
    any_spec = pl.BlockSpec(memory_space=pl.ANY)
    return pl.pallas_call(
        functools.partial(spread_kernel, kind, nodes, edges, rows),
        out_shape=tuple(jax.ShapeDtypeStruct(f.shape, f.dtype) for f in full),
        in_specs=[pl.BlockSpec(memory_space=pltpu.SMEM)] + [any_spec] * 4,
        out_specs=(any_spec,) * 2,
        input_output_aliases={3 + i: i for i in range(2)},
        scratch_shapes=[
            pltpu.VMEM((GRAPHS, edges, width), BF16),
            pltpu.VMEM((GRAPHS, nodes, width), BF16),
            pltpu.VMEM((GRAPHS, edges, width), F32),
            pltpu.VMEM((GRAPHS, nodes, width), F32),
            pltpu.SemaphoreType.DMA((count,)),
            pltpu.SemaphoreType.DMA((count,)),
        ],
        compiler_params=pltpu.CompilerParams(vmem_limit_bytes=24 * 2**20),
        cost_estimate=pl.CostEstimate(flops=0, transcendentals=0, bytes_accessed=12 * (edges + nodes) * width),
        name="spread",
    )(sec, recv_e, recv_n, *full)


def reduce_over_dp(pair, beside):
    devices = lax.axis_size("dp")
    sec = lax.axis_index("section")
    me = lax.axis_index("dp")
    bits = [1 << k for k in range(devices.bit_length() - 1)]
    orders = [bits, bits[:2][::-1] + bits[2:]]
    halved = min(2, len(bits))
    count = [0]

    def swap(part, step):
        pairs = [
            (s * devices + i, s * devices + (i ^ orders[s][step]))
            for s in range(2)
            for i in range(devices)
        ]
        part = part.astype(BF16)
        got = lax.ppermute(part, ("section", "dp"), pairs)
        if count[0] in beside:
            got = beside[count[0]](part, got)
        count[0] += 1
        return got.astype(F32)

    def high(step):
        return jnp.where(sec == 0, me // orders[0][step], me // orders[1][step]) % 2

    terms = pair
    for step in range(halved):
        half = terms[0].shape[0] // 2
        mine = high(step)
        keep = sum(lax.dynamic_slice_in_dim(t, mine * half, half, 0).astype(F32) for t in terms)
        send = sum(lax.dynamic_slice_in_dim(t, (1 - mine) * half, half, 0).astype(F32) for t in terms)
        part = keep + swap(send, step)
        terms = (part,)
    for step in range(halved, len(bits)):
        part = part + swap(part, step)
    for step in reversed(range(halved)):
        got = swap(part, step)
        if step == 0:
            return part, got, high(0)
        part = jnp.where(
            high(step) == 0, jnp.concatenate([part, got], 0), jnp.concatenate([got, part], 0)
        )
    rows = pair[0].shape[0] // 2
    return part[:rows], part[rows:], jnp.zeros((), jnp.int32)


def place_kernel(flag_ref, part_ref, got_ref, *outs):
    own = flag_ref[0] == 0
    rows = part_ref.shape[0]
    at = 0
    for out in outs:
        end = at + out.shape[0]
        if at < rows:
            stop = min(end, rows)
            out[: stop - at, :] = jnp.where(own, part_ref[at:stop, :], got_ref[at:stop, :])
        if end > rows:
            start = max(at, rows)
            here = slice(start - rows, end - rows)
            out[start - at :, :] = jnp.where(own, got_ref[here, :], part_ref[here, :])
        at = end


def place(part, got, flag, sizes):
    vmem = pl.BlockSpec(memory_space=pltpu.VMEM)
    return pl.pallas_call(
        place_kernel,
        out_shape=tuple(jax.ShapeDtypeStruct((rows, part.shape[1]), F32) for rows in sizes),
        in_specs=[pl.BlockSpec(memory_space=pltpu.SMEM), vmem, vmem],
        out_specs=(vmem,) * len(sizes),
        compiler_params=pltpu.CompilerParams(vmem_limit_bytes=16 * 2**20),
        name="place",
    )(flag.reshape(1).astype(jnp.int32), part, got)


def shards(
    node_input,
    edge_input,
    senders,
    receivers,
    node_cot,
    edge_cot,
    edge_w1,
    edge_b1,
    edge_w2,
    edge_b2,
    edge_gain,
    edge_shift,
    node_w1,
    node_b1,
    node_w2,
    node_b2,
    node_gain,
    node_shift,
):
    nodes = node_input.shape[0] // MICRO
    edges = edge_input.shape[0] // MICRO
    width = node_input.shape[1]
    sec = lax.axis_index("section").reshape(1).astype(jnp.int32)
    other = [(0, 1), (1, 0)]
    w_mine = jnp.concatenate([edge_w1[0], edge_w2[0], node_w1[0], node_w2[0]], axis=0)
    v_mine = jnp.concatenate(
        [edge_b1, edge_b2, edge_gain, edge_shift, node_b1, node_b2, node_gain, node_shift], axis=0
    )
    w_theirs = lax.ppermute(w_mine, "section", other)
    v_theirs = lax.ppermute(v_mine, "section", other)
    idx_s = senders.reshape(-1, 128)
    idx_r = receivers.reshape(-1, 128)
    out = run_graphs(
        nodes,
        edges,
        sec,
        idx_s,
        idx_r,
        node_input,
        edge_input,
        node_cot,
        edge_cot,
        w_mine,
        w_theirs,
        v_mine,
        v_theirs,
    )
    full = [out[:2], out[2:4]]
    came = lax.ppermute(out[7], "section", other)
    sent, came = lax.optimization_barrier((out[4:6], came))
    recv = tuple(lax.ppermute(x, "section", other) for x in sent)

    def fill(kind):
        def run(sent, came):
            sent, here, whole = lax.optimization_barrier((sent, recv, full[kind]))
            full[kind] = spread(kind, nodes, edges, sec, *here, whole)
            came, full[kind] = lax.optimization_barrier((came, full[kind]))
            return came

        return run

    total = reduce_over_dp((out[6], came), {3: fill(0), 5: fill(1)})
    (lat_e, lat_n), (gr_e, gr_n) = full
    out = place(*total, (3 * width, width, 2 * width, width) + (1,) * 8)
    w1, w2, n1, n2 = (w[None] for w in out[:4])
    return (
        lat_n[None],
        lat_e[None],
        gr_n[None],
        gr_e[None],
        w1,
        out[4],
        w2,
        out[5],
        out[6],
        out[7],
        n1,
        out[8],
        n2,
        out[9],
        out[10],
        out[11],
    )


def solution(mesh):
    rows = P("dp", None)
    mat = P("section", None, None)
    row = P("section", None)
    in_specs = (rows, rows, P("dp"), P("dp"), rows, rows) + (mat, row, mat, row, row, row) * 2
    whole = P("section", "dp", None)
    out_specs = (whole,) * 4 + (mat, row, mat, row, row, row) * 2
    return jax.shard_map(shards, mesh=mesh, in_specs=in_specs, out_specs=out_specs, check_vma=False)
```

```python
import functools

import jax
import jax.numpy as jnp
from jax import lax
from jax.experimental import pallas as pl
from jax.experimental.pallas import tpu as pltpu
from jax.sharding import PartitionSpec as P

MICRO = 4
GRAPHS = 2
EPS = 1e-05
BLOCK = 256
NODE_BLOCKS = 1
CHUNK = 1024
GRAD_ROWS = 1920
F32 = jnp.float32
BF16 = jnp.bfloat16


def dot(left, right):
    return jnp.dot(left, right, preferred_element_type=F32)


def dot_tn(left, right):
    return lax.dot_general(left, right, (((0,), (0,)), ((), ())), preferred_element_type=F32)


def dot_nt(left, right):
    return lax.dot_general(left, right, (((1,), (1,)), ((), ())), preferred_element_type=F32)


def col_sum(value):
    return jnp.sum(value, axis=0, keepdims=True)


def row_mean(value):
    return jnp.mean(value, axis=1, keepdims=True)


def half_silu(half):
    t = jnp.tanh(half)
    up = 1.0 + t
    act = half * up
    return act, up + act * (1.0 - t)


def twice(lanes):
    return jnp.concatenate([lanes, lanes], axis=1)


def eight_rows(value):
    return jnp.sum(value.reshape(-1, 8, value.shape[1]), axis=0)


def centre(w):
    w = w.astype(F32)
    return (w - row_mean(w)).astype(BF16)


def interleave(parts, skew):
    parts = list(parts)
    done = [False] * len(parts)
    clock = 0
    while not all(done):
        for i, part in enumerate(parts):
            if clock >= i * skew and not done[i]:
                done[i] = next(part, "end") == "end"
        clock += 1


def graphs_kernel(
    nodes,
    edges,
    width,
    sec_ref,
    idx_s,
    idx_r,
    node_hbm,
    edge_hbm,
    ncot_hbm,
    ecot_hbm,
    w_mine,
    w_theirs,
    v_mine,
    v_theirs,
    lat_e,
    lat_n,
    gr_e,
    gr_n,
    send_e,
    send_n,
    wg_keep,
    wg_send,
    es,
    srt,
    cot,
    low,
    act0,
    act1,
    dd0,
    dd1,
    xh0,
    xh1,
    inv0,
    inv1,
    big,
    wv,
    wc,
    vs,
    h0_in,
    cotn,
    nf,
    nlow,
    acc,
    dh_own,
    pw,
    jn,
    act_n,
    slope_n,
    xh_n,
    inv_n,
    wg,
    load_sems,
    big_sems,
    node_sems,
    low_sems,
    nlow_sems,
    grad_sems,
):
    acts, dds, xhs, invs = (act0, act1), (dd0, dd1), (xh0, xh1), (inv0, inv1)
    sec = sec_ref[0]
    first = sec == 0
    n = BLOCK
    rows_n = nodes // NODE_BLOCKS
    node_rows = [slice(i * rows_n, (i + 1) * rows_n) for i in range(NODE_BLOCKS)]
    col_s, col_r, col_1 = width, width + nodes, width + 2 * nodes
    spans = (slice(0, col_1), slice(col_s, col_1 + width))
    own = (slice(0, width), slice(col_1, col_1 + width))
    copy = pltpu.make_async_copy
    rounds = (0, 1, 1, 0)
    full = ((lat_e, lat_n), (lat_e, lat_n), (gr_e, gr_n), (gr_e, gr_n))
    lows = (es.at[:, own[1]], low, low, cot)

    @pl.when(first)
    def _():
        copy(w_mine, wv.at[0], load_sems.at[4]).start()
        copy(w_theirs, wv.at[1], load_sems.at[5]).start()

    @pl.when(jnp.logical_not(first))
    def _():
        copy(w_theirs, wv.at[0], load_sems.at[4]).start()
        copy(w_mine, wv.at[1], load_sems.at[5]).start()

    vs[0] = jnp.where(first, v_mine[...], v_theirs[...])
    vs[1] = jnp.where(first, v_theirs[...], v_mine[...])
    wg[...] = jnp.zeros_like(wg)

    def vec(r, k):
        return vs[r, k : k + 1, :]

    def weights(r):
        w1 = [wv[r, k * width : (k + 1) * width, :] for k in range(3)]
        at = 3 * width
        return (
            w1[0],
            jnp.concatenate(w1[1:], axis=1),
            wv[r, at : at + width, :],
            wv[r, at + width : at + 3 * width, :],
            wv[r, at + 3 * width : at + 4 * width, :],
        )

    def put_w(r, at, value):
        here = slice(at, at + value.shape[0])
        wg[r, here, :] = wg[r, here, :] + value

    def put_v(r, k, value):
        put_w(r, 7 * width + k, value)

    def graph(which, carry):
        gi = 2 * sec + which
        other = 2 * (1 - sec) + which
        erow = pl.multiple_of(gi * edges, edges)
        nrow = pl.multiple_of(gi * nodes, nodes)

        def big_copy(phase, k):
            at = pl.multiple_of(jnp.where(sec == rounds[phase], gi, other) * edges, edges) + k * CHUNK
            here = pl.ds(pl.multiple_of(at, CHUNK), CHUNK)
            return copy(big.at[pl.ds(k * CHUNK, CHUNK)], full[phase][0].at[here], big_sems.at[k])

        def big_wait(phase):
            for k in range(edges // CHUNK):
                big_copy(phase, k).wait()

        def node_copy(phase):
            at = pl.multiple_of(jnp.where(sec == rounds[phase], gi, other) * nodes, nodes)
            return copy(nf.at[phase % 2], full[phase][1].at[pl.ds(at, nodes)], node_sems.at[phase])

        def low_copies(phase):
            kind = jnp.where(sec == 0, 0, 1) if phase == 1 else phase // 2
            return (
                copy(lows[phase], send_e.at[kind, which], low_sems.at[phase]),
                copy(nlow.at[phase % 2], send_n.at[kind, which], nlow_sems.at[phase]),
            )

        def low_start(phase, k):
            if phase > 0 and (phase, k) != (2, 0):
                low_copies(phase - 1)[k].wait()
            if phase < 3:
                low_copies(phase)[k].start()
            else:

                @pl.when(sec != rounds[phase])
                def _():
                    low_copies(phase)[k].start()

        def nodes_out(phase, here, out):
            nf[phase % 2, here, :] = out
            nlow[phase % 2, here, :] = out.astype(BF16)

        def drain():
            big_wait(3)
            for phase in (2, 3):
                node_copy(phase).wait()

            @pl.when(sec != rounds[3])
            def _():
                for c in low_copies(3):
                    c.wait()

        loads = [
            copy(edge_hbm.at[pl.ds(erow, edges)], es.at[:, own[0]], load_sems.at[0]),
            copy(node_hbm.at[pl.ds(nrow, nodes)], h0_in, load_sems.at[1]),
            copy(ncot_hbm.at[pl.ds(nrow, nodes)], cotn, load_sems.at[3]),
        ]
        load_cot = copy(ecot_hbm.at[pl.ds(erow, edges)], cot, load_sems.at[2])
        for c in loads:
            c.start()

        rows = edges // 128
        irow = pl.multiple_of(gi * rows, rows)

        one, zero = jnp.ones((128, 128), BF16), jnp.zeros((128, 128), BF16)

        def build(j):
            at = slice(j * 128, (j + 1) * 128)
            for k, idx in enumerate((idx_s, idx_r)):
                row = idx[pl.ds(irow + j, 1), :]
                ahead = jnp.broadcast_to(row, (16, 128)) - lax.broadcasted_iota(jnp.int32, (16, 128), 0)
                ahead = ahead.astype(jnp.int16)
                for c in range(0, nodes, 16):
                    hit = jnp.where(ahead == jnp.int16(c), one[:16], zero[:16])
                    srt[k * nodes + c : k * nodes + c + 16, at] = hit
                column = jnp.broadcast_to(row, (128, 128)).T
                ahead = (column - lax.broadcasted_iota(jnp.int32, (128, 128), 1)).astype(jnp.int16)
                for c in range(0, nodes, 128):
                    to = col_s + k * nodes + c
                    es[at, to : to + 128] = jnp.where(ahead == jnp.int16(c), one, zero)

        @pl.when(which == 0)
        def _():
            copy(w_mine, wv.at[0], load_sems.at[4]).wait()
            copy(w_mine, wv.at[1], load_sems.at[5]).wait()
            for r in range(2):
                we, _, w2, _, w4 = weights(r)
                wc[r, :width, :] = centre(w2)
                wc[r, width : 2 * width, :] = centre(w4)
                wc[r, 2 * width : 3 * width, :] = (w2.astype(F32) * 0.5).T.astype(BF16)
                wc[r, 3 * width :, :] = we.astype(F32).T.astype(BF16)

        @pl.when(which > 0)
        def _():
            drain()

        for c in loads:
            c.wait()

        def forward_table(r, here, h):
            _, wsr, _, _, _ = weights(r)
            hl = h.astype(BF16)
            jn[r, here, :width] = hl
            k_s = width if r == 0 else 0
            table = dot(hl, wsr) * 0.5
            pw[k_s + here.start : k_s + here.stop, :] = table[:, :width].astype(BF16)
            to = k_s + nodes
            pw[to + here.start : to + here.stop, :] = (table[:, width:] + vec(r, 0) * 0.5).astype(BF16)

        def forward(r, h):
            phase = r
            we, _, _, w3, _ = weights(r)
            k_e = 0 if r == 0 else 2 * nodes
            pw[k_e : k_e + width, :] = we * 0.5
            if r == 0:
                for here in node_rows:
                    forward_table(0, here, h(here))
            b2 = vec(r, 1)
            b2c = b2 - row_mean(b2)
            gain, shift = vec(r, 2), vec(r, 3)
            lo = lows[phase]
            message = (xh1, cot)[r]
            if phase > 0:
                big_wait(phase - 1)

            def block(i):
                here = slice(i * n, (i + 1) * n)
                if r == 0:
                    for j in range(i * n // 128, (i + 1) * n // 128):
                        build(j)
                    yield
                half = dot(es[here, spans[r]], pw[...])
                yield
                act, slope = half_silu(half)
                act = act.astype(BF16)
                acts[r][:, here] = act.T
                dds[r][here, :] = slope.astype(BF16)
                yield
                z = dot(act, wc[r, :width, :])
                yield
                z = z + b2c
                inv = lax.rsqrt(row_mean(z * z) + EPS)
                xh = z * inv
                xhs[r][here, :] = xh.astype(BF16)
                invs[r][here, :] = jnp.broadcast_to(inv, (n, 128)).astype(BF16)
                update = xh * gain + shift
                message[here, :] = update.astype(BF16)
                out = es[here, own[r]].astype(F32) + update
                big[here, :] = out
                lo[here, :] = out.astype(BF16)
                yield
                if (i + 1) * n % CHUNK == 0:
                    part = slice((i + 1) * n - CHUNK, (i + 1) * n)
                    big_copy(phase, i * n // CHUNK).start()
                    add = dot(srt[nodes:, part], message[part, :])
                    acc[:nodes, :] = add if part.start == 0 else acc[:nodes, :] + add
                    yield

            interleave([block(i) for i in range(edges // n)], 1)
            low_start(phase, 0)
            if r == 1:
                load_cot.start()
            b4 = vec(r, 5)
            b4c = b4 - row_mean(b4)
            b3 = vec(r, 4)

            def node_block(here):
                jn[r, here, width:] = acc[here, :].astype(BF16)
                z = dot(jn[r, here, :], w3)
                yield
                act, slope = half_silu((z + b3) * 0.5)
                act = act.astype(BF16)
                act_n[r, here, :] = act
                slope_n[r, here, :] = slope.astype(BF16)
                z = dot(act, wc[r, width : 2 * width, :])
                yield
                z = z + b4c
                inv = lax.rsqrt(row_mean(z * z) + EPS)
                xh = z * inv
                xh_n[r, here, :] = xh.astype(BF16)
                inv_n[r, here, :] = jnp.broadcast_to(inv, (rows_n, 128))
                out = h(here) + xh * vec(r, 6) + vec(r, 7)
                nodes_out(phase, here, out)
                if r == 0:
                    forward_table(1, here, out)
                yield

            interleave([node_block(here) for here in node_rows], 1)
            node_copy(phase).start()
            low_start(phase, 1)

        def backward(r, de_ref, dn_rows, before):
            phase = 3 - r
            _, wsr, _, w3, w4 = weights(r)
            gain_n = vec(r, 6)
            dns, d4s, d3s, djs = [], [], [], []

            def node_block(here):
                dn = dn_rows(here)
                dns.append(dn)
                yield
                xh = xh_n[r, here, :].astype(F32)
                g = dn * gain_n
                d4 = twice(inv_n[r, here, :]) * (g - row_mean(g) - xh * row_mean(g * xh))
                d4s.append(d4.astype(BF16))
                d3 = dot_nt(d4s[-1], w4)
                yield
                d3s.append((d3 * slope_n[r, here, :].astype(F32) * 0.5).astype(BF16))
                djn = dot_nt(d3s[-1], w3)
                yield
                djs.append(djn[:, width:].astype(BF16))
                dh_own[here, :] = djn[:, :width]
                yield

            interleave([node_block(here) for here in node_rows], 1)
            if phase == 3:
                node_copy(2).start()
                low_start(2, 1)
            for job in before:
                job()
            dtotal, d4, d3, dn = (jnp.concatenate(x, axis=0) for x in (djs, d4s, d3s, dns))
            put_w(r, 6 * width, dot_tn(act_n[r], d4))
            put_w(r, 4 * width, dot_tn(jn[r], d3))
            put_v(r, 6, col_sum(dn * xh_n[r].astype(F32)))
            put_v(r, 7, col_sum(dn))
            put_v(r, 5, col_sum(d4.astype(F32)))
            put_v(r, 4, col_sum(d3.astype(F32)))
            gain = vec(r, 2)
            w2t = wc[r, 2 * width : 3 * width, :]
            wet = wc[r, 3 * width :, :]
            lo = lows[phase]
            sums = [jnp.zeros((8, width), F32)] * 3
            big_wait(phase - 1)

            def block(i):
                here = slice(i * n, (i + 1) * n)
                g = dot(es[here, col_r:col_1], dtotal)
                yield
                xh = xhs[r][here, :].astype(F32)
                inv = twice(invs[r][here, :].astype(F32))
                g = (de_ref[here, :].astype(F32) + g) * gain
                gx = g * xh
                d2 = inv * (g - row_mean(g) - xh * row_mean(gx))
                for k, value in enumerate((gx, g, d2)):
                    sums[k] = sums[k] + eight_rows(value)
                d2 = d2.astype(BF16)
                xhs[r][here, :] = d2
                yield
                d1 = dot(d2, w2t)
                yield
                d1 = (d1 * dds[r][here, :].astype(F32)).astype(BF16)
                dds[r][here, :] = d1
                yield
                back = dot(d1, wet)
                yield
                out = de_ref[here, :].astype(F32) + back
                big[here, :] = out
                lo[here, :] = out.astype(BF16)
                yield
                if (i + 1) * n % CHUNK == 0:
                    part = slice((i + 1) * n - CHUNK, (i + 1) * n)
                    big_copy(phase, i * n // CHUNK).start()
                    put_w(r, 3 * width, dot(acts[r][:, part], xhs[r][part, :]))
                    yield
                    for half in (slice(0, nodes), slice(nodes, 2 * nodes)):
                        add = dot(srt[half, part], dds[r][part, :])
                        acc[half, :] = add if part.start == 0 else acc[half, :] + add
                        yield
                    put_w(r, 0, dot_tn(es[part, own[r]], dds[r][part, :]))
                    yield

            interleave([block(i) for i in range(edges // n)], 1)
            low_start(phase, 0)
            both = jnp.concatenate([acc[:nodes, :], acc[nodes:, :]], axis=1).astype(BF16)
            node_copy(phase - 2).wait()

            def dn_out(here):
                out = dn_rows(here, True) + dh_own[here, :] + dot_nt(both[here, :], wsr)
                nodes_out(phase, here, out)
                return out

            def sums_out():
                put_v(r, 2, col_sum(sums[0]) / gain)
                put_v(r, 3, col_sum(sums[1]) / gain)
                put_v(r, 1, col_sum(sums[2]))
                put_v(r, 0, col_sum(both[:, width:].astype(F32)))

            def table_out():
                dws = dot_tn(jn[r, :, :width], both)
                put_w(r, width, dws[:, :width])
                put_w(r, 2 * width, dws[:, width:])

            return dn_out, (sums_out, table_out)

        forward(0, lambda here: h0_in[here, :].astype(F32))
        forward(1, lambda here: nf[0, here, :])
        load_cot.wait()
        low_copies(1)[0].wait()
        dn_out, jobs = backward(1, cot, lambda here, again=False: cotn[here, :].astype(F32), ())
        last = lambda here, again=False: nf[0, here, :] if again else dn_out(here)
        dn_out, jobs = backward(0, low, last, jobs)
        for here in node_rows:
            dn_out(here)
        node_copy(3).start()
        low_start(3, 1)
        for job in jobs:
            job()

        @pl.when(which == GRAPHS - 1)
        def _():
            drain()

        return carry

    lax.fori_loop(0, GRAPHS, graph, 0)
    wl = dd0.at[:GRAD_ROWS]

    for r in range(2):

        @pl.when(sec == r)
        def _(r=r):
            copy(wg.at[r], wg_keep, grad_sems.at[0]).start()

        @pl.when(sec != r)
        def _(r=r):
            wl[...] = wg[r].astype(BF16)
            copy(wl, wg_send, grad_sems.at[1]).start()

    copy(wg.at[0], wg_keep, grad_sems.at[0]).wait()
    copy(wl, wg_send, grad_sems.at[1]).wait()


def run_graphs(nodes, edges, sec, idx_s, idx_r, node, edge, ncot, ecot, w_mine, w_theirs, v_mine, v_theirs):
    width = node.shape[1]
    any_spec = pl.BlockSpec(memory_space=pl.ANY)
    vmem = pl.BlockSpec(memory_space=pltpu.VMEM)
    smem = pl.BlockSpec(memory_space=pltpu.SMEM)
    shape = jax.ShapeDtypeStruct
    whole = [shape((edge.shape[0], width), F32), shape((node.shape[0], width), F32)]
    outs = (
        *whole,
        *whole,
        shape((2, GRAPHS, edges, width), BF16),
        shape((2, GRAPHS, nodes, width), BF16),
        shape((GRAD_ROWS, width), F32),
        shape((GRAD_ROWS, width), BF16),
    )
    return pl.pallas_call(
        functools.partial(graphs_kernel, nodes, edges, width),
        out_shape=outs,
        in_specs=[smem, vmem, vmem] + [any_spec] * 6 + [vmem, vmem],
        out_specs=(any_spec,) * 8,
        scratch_shapes=[
            pltpu.VMEM((edges, 2 * width + 2 * nodes), BF16),
            pltpu.VMEM((2 * nodes, edges), BF16),
            *[pltpu.VMEM((edges, width), BF16)] * 2,
            *[pltpu.VMEM((width, edges), BF16)] * 2,
            *[pltpu.VMEM((edges, width), BF16)] * 4,
            *[pltpu.VMEM((edges, 128), BF16)] * 2,
            pltpu.VMEM((edges, width), F32),
            pltpu.VMEM((2, w_mine.shape[0], width), BF16),
            pltpu.VMEM((2, 4 * width, width), BF16),
            pltpu.VMEM((2, 8, width), F32),
            pltpu.VMEM((nodes, width), BF16),
            pltpu.VMEM((nodes, width), BF16),
            pltpu.VMEM((2, nodes, width), F32),
            pltpu.VMEM((2, nodes, width), BF16),
            pltpu.VMEM((2 * nodes, width), F32),
            pltpu.VMEM((nodes, width), F32),
            pltpu.VMEM((2 * nodes + width, width), BF16),
            pltpu.VMEM((2, nodes, 2 * width), BF16),
            *[pltpu.VMEM((2, nodes, width), BF16)] * 3,
            pltpu.VMEM((2, nodes, 128), F32),
            pltpu.VMEM((2, GRAD_ROWS, width), F32),
            pltpu.SemaphoreType.DMA((8,)),
            pltpu.SemaphoreType.DMA((edges // CHUNK,)),
            *[pltpu.SemaphoreType.DMA((4,))] * 3,
            pltpu.SemaphoreType.DMA((2,)),
        ],
        compiler_params=pltpu.CompilerParams(vmem_limit_bytes=60 * 2**20),
        cost_estimate=pl.CostEstimate(flops=80 * 2 * edges * width * width, transcendentals=0, bytes_accessed=2**25),
        name="graphs",
    )(sec, idx_s, idx_r, node, edge, ncot, ecot, w_mine, w_theirs, v_mine, v_theirs)


def spread_kernel(kind, nodes, edges, rows, sec_ref, recv_e, recv_n, *rest):
    out_e, out_n, e_in, n_in, e_out, n_out, in_sems, out_sems = rest[2:]
    start = GRAPHS * (1 - sec_ref[0])
    parts = []
    for g in range(GRAPHS):
        at = pl.multiple_of((start + g) * nodes, nodes)
        parts.append((recv_n.at[kind, g], n_in.at[g], n_out.at[g], out_n.at[pl.ds(at, nodes)]))
        for i in range(edges // rows):
            here = pl.ds(i * rows, rows)
            at = pl.multiple_of((start + g) * edges + i * rows, rows)
            parts.append((recv_e.at[kind, g, here], e_in.at[g, here], e_out.at[g, here], out_e.at[pl.ds(at, rows)]))
    reads = [pltpu.make_async_copy(p[0], p[1], in_sems.at[i]) for i, p in enumerate(parts)]
    writes = [pltpu.make_async_copy(p[2], p[3], out_sems.at[i]) for i, p in enumerate(parts)]
    for c in reads:
        c.start()
    for p, r, w in zip(parts, reads, writes):
        r.wait()
        p[2][...] = p[1][...].astype(F32)
        w.start()
    for w in writes:
        w.wait()


def spread(kind, nodes, edges, sec, recv_e, recv_n, full):
    width = recv_e.shape[-1]
    rows = 1024
    count = GRAPHS * (edges // rows + 1)
    any_spec = pl.BlockSpec(memory_space=pl.ANY)
    return pl.pallas_call(
        functools.partial(spread_kernel, kind, nodes, edges, rows),
        out_shape=tuple(jax.ShapeDtypeStruct(f.shape, f.dtype) for f in full),
        in_specs=[pl.BlockSpec(memory_space=pltpu.SMEM)] + [any_spec] * 4,
        out_specs=(any_spec,) * 2,
        input_output_aliases={3 + i: i for i in range(2)},
        scratch_shapes=[
            pltpu.VMEM((GRAPHS, edges, width), BF16),
            pltpu.VMEM((GRAPHS, nodes, width), BF16),
            pltpu.VMEM((GRAPHS, edges, width), F32),
            pltpu.VMEM((GRAPHS, nodes, width), F32),
            pltpu.SemaphoreType.DMA((count,)),
            pltpu.SemaphoreType.DMA((count,)),
        ],
        compiler_params=pltpu.CompilerParams(vmem_limit_bytes=24 * 2**20),
        cost_estimate=pl.CostEstimate(flops=0, transcendentals=0, bytes_accessed=12 * (edges + nodes) * width),
        name="spread",
    )(sec, recv_e, recv_n, *full)


def reduce_over_dp(pair, beside):
    devices = lax.axis_size("dp")
    me = lax.axis_index("dp")
    count = [0]

    def swap(parts, hops):
        got = [
            lax.ppermute(p.astype(BF16), "dp", [(i, i ^ hop) for i in range(devices)])
            for p, hop in zip(parts, hops)
        ]
        if count[0] in beside:
            got[-1] = beside[count[0]](parts[-1], got[-1])
        count[0] += 1
        return got

    def scatter(terms, step):
        place_of = (me // step) % 4
        rows = terms[0].shape[0] // 4

        def quarter(k):
            at = (place_of ^ k) * rows
            return sum(lax.dynamic_slice_in_dim(t, at, rows, 0).astype(F32) for t in terms)

        got = swap([quarter(k) for k in (3, 1, 2)], (3 * step, step, 2 * step))
        return quarter(0) + sum(g.astype(F32) for g in got)

    part = scatter(pair, 1)
    if devices >= 16:
        part = scatter((part,), 4)
    hop = 16 if devices >= 16 else 4
    while hop < devices:
        part = part + swap([part], (hop,))[0].astype(F32)
        hop *= 2
    part = part.astype(BF16)
    if devices >= 16:
        place_of = (me // 4) % 4
        diagonal, one, two = swap([part] * 3, (12, 4, 8))
        stack = jnp.stack([part, one, two, diagonal])
        part = jnp.concatenate(
            [lax.dynamic_index_in_dim(stack, place_of ^ q, 0, keepdims=False) for q in range(4)], axis=0
        )
    diagonal, one, two = swap([part] * 3, (3, 1, 2))
    return (part, one, two, diagonal), me % 4


def place_kernel(place_ref, *refs):
    quarters, outs = refs[:4], refs[4:]
    mine = place_ref[0]
    rows = quarters[0].shape[0]
    start = 0
    for out in outs:
        end = start + out.shape[0]
        for q in range(4):
            at, stop = max(start, q * rows), min(end, (q + 1) * rows)
            if at < stop:
                here = slice(at - q * rows, stop - q * rows)
                value = quarters[q][here, :]
                for p in range(1, 4):
                    value = jnp.where(mine == p, quarters[q ^ p][here, :], value)
                out[at - start : stop - start, :] = value
        start = end


def place(quarters, place_of, sizes):
    vmem = pl.BlockSpec(memory_space=pltpu.VMEM)
    return pl.pallas_call(
        place_kernel,
        out_shape=tuple(jax.ShapeDtypeStruct((rows, quarters[0].shape[1]), F32) for rows in sizes),
        in_specs=[pl.BlockSpec(memory_space=pltpu.SMEM)] + [vmem] * 4,
        out_specs=(vmem,) * len(sizes),
        compiler_params=pltpu.CompilerParams(vmem_limit_bytes=16 * 2**20),
        name="place",
    )(place_of.reshape(1).astype(jnp.int32), *(q.astype(F32) for q in quarters))


def shards(
    node_input,
    edge_input,
    senders,
    receivers,
    node_cot,
    edge_cot,
    edge_w1,
    edge_b1,
    edge_w2,
    edge_b2,
    edge_gain,
    edge_shift,
    node_w1,
    node_b1,
    node_w2,
    node_b2,
    node_gain,
    node_shift,
):
    nodes = node_input.shape[0] // MICRO
    edges = edge_input.shape[0] // MICRO
    width = node_input.shape[1]
    sec = lax.axis_index("section").reshape(1).astype(jnp.int32)
    other = [(0, 1), (1, 0)]
    w_mine = jnp.concatenate([edge_w1[0], edge_w2[0], node_w1[0], node_w2[0]], axis=0)
    v_mine = jnp.concatenate(
        [edge_b1, edge_b2, edge_gain, edge_shift, node_b1, node_b2, node_gain, node_shift], axis=0
    )
    w_theirs = lax.ppermute(w_mine, "section", other)
    v_theirs = lax.ppermute(v_mine, "section", other)
    idx_s = senders.reshape(-1, 128)
    idx_r = receivers.reshape(-1, 128)
    out = run_graphs(
        nodes,
        edges,
        sec,
        idx_s,
        idx_r,
        node_input,
        edge_input,
        node_cot,
        edge_cot,
        w_mine,
        w_theirs,
        v_mine,
        v_theirs,
    )
    full = [out[:2], out[2:4]]
    came = lax.ppermute(out[7], "section", other)
    sent, came = lax.optimization_barrier((out[4:6], came))
    recv = tuple(lax.ppermute(x, "section", other) for x in sent)

    def fill(kind):
        def run(sent, came):
            sent, here, whole = lax.optimization_barrier((sent, recv, full[kind]))
            full[kind] = spread(kind, nodes, edges, sec, *here, whole)
            came, full[kind] = lax.optimization_barrier((came, full[kind]))
            return came

        return run

    quarters, place_of = reduce_over_dp((out[6], came), {2: fill(0), 3: fill(1)})
    (lat_e, lat_n), (gr_e, gr_n) = full
    out = place(quarters, place_of, (3 * width, width, 2 * width, width) + (1,) * 8)
    w1, w2, n1, n2 = (w[None] for w in out[:4])
    return (
        lat_n[None],
        lat_e[None],
        gr_n[None],
        gr_e[None],
        w1,
        out[4],
        w2,
        out[5],
        out[6],
        out[7],
        n1,
        out[8],
        n2,
        out[9],
        out[10],
        out[11],
    )


def solution(mesh):
    rows = P("dp", None)
    mat = P("section", None, None)
    row = P("section", None)
    in_specs = (rows, rows, P("dp"), P("dp"), rows, rows) + (mat, row, mat, row, row, row) * 2
    whole = P("section", "dp", None)
    out_specs = (whole,) * 4 + (mat, row, mat, row, row, row) * 2
    return jax.shard_map(shards, mesh=mesh, in_specs=in_specs, out_specs=out_specs, check_vma=False)
```
